32 devices in a mesh: grp: 4 (over y, core), exp: 8 (over z, x).
Axes of the slice: x: 2, y: 2, z: 4, core: 2. Of those that a mesh axis runs over, the one named last changes fastest.
Arguments:
- attention_rows: bfloat16 [8, 2048, 2048], P('exp', None, 'grp'), may hold values from -6 to 6
- expert_choice: int32 [8, 2048, 2], P('exp', 'grp'), may hold values from 0 to 15, all different within a row; in each aligned block of 512 rows (0 to 511, 512 to 1023, ..., all dimensions but the last counted through in order) at most 96 rows name the same one
- gate_weights: float32 [8, 2048, 2], P('exp', 'grp'), may hold values from 0.05 to 1
- up_blocks: int32 [16, 32, 2], P('exp'), may hold values from 0 to 15, as said below
- up_values: bfloat16 [16, 32, 2, 128, 128], P('exp'), may hold values from -0.375 to 0.375
- down_blocks: int32 [16, 16, 4], P('exp'), may hold values from 0 to 31, as said below
- down_values: bfloat16 [16, 16, 4, 128, 128], P('exp'), may hold values from -0.25 to 0.25
Outputs:
- moe_out: bfloat16 [8, 2048, 2048], P('exp', 'grp')
The draws below stay inside these ranges and needn't reach their ends.
Inputs may be any that keep to these rules, and one draw needn't show every extreme that they name: `expert_choice`: each token names two different experts; among the 512 tokens of one device no expert is named by more than 96 tokens, and in some device one expert is named by exactly 96. `up_blocks`: for each expert and each block column, 2 different block rows. `down_blocks`: for each expert and each block column, 4 different block rows.
All inputs are finite; a program needn't handle non-finite values.
Results may differ from the reference program's by a relative error of at most 0.0057.
Values may be sent and summed in bfloat16 or wider, within the bound.
No kernel may reach another device: no remote copies, remote signals or barrier semaphores. Data moves between devices by JAX's collectives and lax.ppermute only.
A program may use at most 128 MiB of HBM per device.

```python
import math
import jax
import jax.numpy as jnp
import numpy as np
from jax import lax

D = 2048
FF = 4096
BLK = 128
KPC_UP = 2
KPC_DOWN = 4
TOK_DEV = 512
ROWS_BLK = 2048
TOKENS = 16384
EXPERTS = 16
CAP = 96
N_EXP = 8


def draw_up_blocks(key, part):
    key_list = jax.random.split(jax.random.fold_in(key, 11), EXPERTS * (FF // BLK))
    picked = jax.vmap(lambda one_key: jax.random.permutation(one_key, D // BLK)[:KPC_UP])(key_list)
    return picked.reshape(EXPERTS, FF // BLK, KPC_UP).astype(jnp.int32)


def draw_down_blocks(key, part):
    key_list = jax.random.split(jax.random.fold_in(key, 23), EXPERTS * (D // BLK))
    picked = jax.vmap(lambda one_key: jax.random.permutation(one_key, FF // BLK)[:KPC_DOWN])(key_list)
    return picked.reshape(EXPERTS, D // BLK, KPC_DOWN).astype(jnp.int32)


def block_scale(stream_key, dims, cuts, least, high):
    factor_of = 1.0
    for axis_at, blocks in cuts:
        heights = jax.random.uniform(jax.random.fold_in(jax.random.fold_in(stream_key, 6), axis_at), (blocks,), jnp.float32, least / len(cuts), high / len(cuts))
        factor_of = factor_of * jnp.repeat(jnp.exp(heights), dims[axis_at] // blocks).reshape((-1,) + (1,) * (len(dims) - 1 - axis_at))
    return factor_of


def routed_block(key, own, number, rows, amount, top, limit, slope):
    ranking = jax.random.permutation(key, amount)
    packed, ordinary = load_shares(amount, rows * top, limit, slope, True), load_shares(amount, rows * top, limit, slope, False)
    places = jnp.arange(amount)

    def named(sizes, turn):
        used = int((sizes > 0).sum())
        fixed = max(1, used // 4)
        shifted = fixed + (places - fixed + turn * (used - fixed)) % max(1, amount - fixed)
        return jnp.zeros((amount,), jnp.int32).at[ranking[jnp.where(places < fixed, places, shifted)]].set(jnp.asarray(sizes, jnp.int32))

    sizes = jnp.where(number % 4 == 0, named(packed, number // 4), named(ordinary, number - number // 4 - 1))
    mixed = jax.random.permutation(jax.random.fold_in(own, 3), amount)
    source_of, sink = mixed[0:amount // 2 * 2:2], mixed[1:amount // 2 * 2:2]
    room = jnp.minimum(sizes[source_of] - 1, limit - sizes[sink]) // 2
    room = jnp.where((source_of == ranking[0]) | (sink == ranking[0]) | (sizes[sink] == 0), 0, jnp.maximum(room, 0))
    shifted = jax.random.randint(jax.random.fold_in(own, 4), (amount // 2,), 0, 1 << 20) % (room + 1)
    sizes = sizes.at[source_of].add(-shifted).at[sink].add(shifted)
    items = jnp.searchsorted(jnp.cumsum(sizes), jnp.arange(rows * top), side="right").astype(jnp.int32)
    table = items.reshape(top, rows).T
    table = table[jax.random.permutation(jax.random.fold_in(own, 1), rows)]
    turn = jax.random.randint(jax.random.fold_in(own, 2), (rows, 1), 0, top)
    return jnp.take_along_axis(table, (jnp.arange(top)[None, :] + turn) % top, axis=1)


def load_shares(number_of, total, reach, skew, full):
    weights = [(1 << 20) // math.isqrt(rank ** skew) + 1 for rank in range(1, number_of + 1)]
    largest = reach if full else min(reach, max(-(-total // number_of), total * weights[0] // sum(weights)))
    least = 1 if total - largest >= number_of - 1 else 0
    holding, surplus = [largest] + [least] * (number_of - 1), total - largest - least * (number_of - 1)
    while surplus > 0:
        movable = [i for i in range(1, number_of) if holding[i] < largest] or [i for i in range(1, number_of) if holding[i] < reach]
        whole, left = sum([weights[i] for i in movable]), surplus
        for i in movable:
            more = min(reach - holding[i], max(1, left * weights[i] // whole), surplus)
            holding[i] = holding[i] + more
            surplus = surplus - more
    return np.array(holding)


def scatter_about(own_key, shape, deviation, reach, cuts=(), kind=jnp.bfloat16):
    gain = block_scale(own_key, shape, cuts, -0.22, 0.18) if cuts else 1.0
    values = jax.random.normal(own_key, shape, jnp.float32) * deviation * gain
    return jnp.minimum(jnp.maximum(values, -reach), reach).astype(kind)


def setup_inputs(seed: int = 0) -> dict:
    arg_keys = jax.random.split(jax.random.key(seed), 8)
    attention_rows = scatter_about(arg_keys[0], (N_EXP, ROWS_BLK, D), 1.0, 6.0, ((0, 8), (2, 4)))
    expert_choice_keys = jax.random.split(jax.random.fold_in(arg_keys[1], 1), N_EXP * ROWS_BLK // TOK_DEV)
    expert_choice_turns = jax.random.permutation(jax.random.fold_in(arg_keys[1], 3), N_EXP * ROWS_BLK // TOK_DEV)
    expert_choice = jax.vmap(lambda own, number: routed_block(jax.random.fold_in(arg_keys[1], 2), own, number, TOK_DEV, EXPERTS, 2, CAP, 1))(expert_choice_keys, expert_choice_turns).reshape((N_EXP, ROWS_BLK, 2))
    gate_weights = jnp.clip(0.05 + 0.95 * jax.random.uniform(arg_keys[2], (N_EXP, ROWS_BLK, 2), jnp.float32) ** block_scale(arg_keys[2], (N_EXP, ROWS_BLK, 2), ((0, 8), (1, 4)), -0.2, 0.2), 0.05, 1.0)
    up_blocks = draw_up_blocks(jax.random.fold_in(arg_keys[7], 71), 0)
    up_values = scatter_about(arg_keys[4], (EXPERTS, FF // BLK, KPC_UP, BLK, BLK), (KPC_UP * BLK) ** -0.5, 0.375, ((0, 8),))
    down_blocks = draw_down_blocks(jax.random.fold_in(arg_keys[7], 71), 0)
    down_values = scatter_about(arg_keys[6], (EXPERTS, D // BLK, KPC_DOWN, BLK, BLK), (KPC_DOWN * BLK) ** -0.5, 0.25, ((0, 8),))
    return {"attention_rows": attention_rows, "expert_choice": expert_choice, "gate_weights": gate_weights, "up_blocks": up_blocks, "up_values": up_values, "down_blocks": down_blocks, "down_values": down_values}


def block_ffn(token_rows, up_rows, up_vals, down_rows, down_vals):
    row_count = token_rows.shape[0]
    blocks_in = token_rows.astype(jnp.float32).reshape(row_count, D // BLK, BLK)
    chosen = blocks_in[:, up_rows]
    hidden = jnp.einsum("rcib,cibd->rcd", chosen, up_vals.astype(jnp.float32), precision=lax.Precision.HIGHEST)
    hidden = jax.nn.gelu(hidden, approximate=True).astype(jnp.bfloat16)
    hidden = lax.optimization_barrier(hidden).astype(jnp.float32)
    chosen_mid = hidden[:, down_rows]
    result = jnp.einsum("rjib,jibd->rjd", chosen_mid, down_vals.astype(jnp.float32), precision=lax.Precision.HIGHEST)
    return result.reshape(row_count, D).astype(jnp.bfloat16)


def reference(attention_rows, expert_choice, gate_weights, up_blocks, up_values, down_blocks, down_values):
    tile_rows = 512
    flat_rows = attention_rows.reshape(TOKENS, D)
    pair_ids = expert_choice.reshape(TOKENS * 2).astype(jnp.int32)
    pair_gates = gate_weights.reshape(TOKENS * 2)
    order_index = jnp.argsort(pair_ids, stable=True).astype(jnp.int32)
    padded_order = jnp.concatenate([order_index, jnp.zeros((tile_rows,), jnp.int32)])
    counts = jax.ops.segment_sum(jnp.ones_like(pair_ids), pair_ids, num_segments=EXPERTS).astype(jnp.int32)
    offsets = (jnp.cumsum(counts) - counts).astype(jnp.int32)

    def per_expert(expert_index, running):
        up_rows = up_blocks[expert_index]
        up_vals = up_values[expert_index]
        down_rows = down_blocks[expert_index]
        down_vals = down_values[expert_index]
        expert_count = counts[expert_index]
        expert_start = offsets[expert_index]

        def per_tile(tile_index, acc_rows):
            first_pos = (expert_start + tile_index * tile_rows).astype(jnp.int32)
            pair_slice = lax.dynamic_slice_in_dim(padded_order, first_pos, tile_rows, 0)
            valid = (tile_index * tile_rows + jnp.arange(tile_rows, dtype=jnp.int32)) < expert_count
            token_index = pair_slice // 2
            rows_here = flat_rows[token_index]
            out_rows = block_ffn(rows_here, up_rows, up_vals, down_rows, down_vals)
            out_wide = lax.optimization_barrier(out_rows).astype(jnp.float32)
            weight_here = jnp.where(valid, pair_gates[pair_slice], jnp.zeros((), jnp.float32))
            return acc_rows.at[token_index].add(weight_here[:, None] * out_wide)

        tile_count = (expert_count + tile_rows - 1) // tile_rows
        return lax.fori_loop(0, tile_count, per_tile, running)

    total = lax.fori_loop(0, EXPERTS, per_expert, jnp.zeros((TOKENS, D), jnp.float32))
    return total.astype(jnp.bfloat16).reshape(N_EXP, ROWS_BLK, D)
```

```python
import functools
import math

import jax
import jax.numpy as jnp
import numpy as np
from jax import lax
from jax.experimental import pallas as pl
from jax.experimental.pallas import tpu as pltpu
from jax.sharding import PartitionSpec as P

AXES = ("grp", "exp")


def place(core, plane):
    return jnp.where(plane < 2, core, 3 - core)


def all_pairs(rule):
    pairs = []
    for y in range(2):
        for core in range(2):
            for z in range(4):
                for x in range(2):
                    to = rule(y, core, z, x)
                    if to is not None:
                        ty, tc, tz, tx = to
                        pairs.append(((y * 2 + core) * 8 + z * 2 + x, (ty * 2 + tc) * 8 + tz * 2 + tx))
    return pairs


def along_z(step, senders):
    return all_pairs(lambda y, c, z, x: (y, c, z + step, x) if (z, c) in senders else None)


def peer_pairs(other_x, k):
    return all_pairs(lambda y, c, z, x: (y ^ (k >> 1), c ^ (k & 1), z, x ^ other_x))


def send(value, pairs):
    return lax.ppermute(value, AXES, pairs)


def after(value, other):
    return lax.optimization_barrier((value, other))[0]


TABLE_ROWS = 48


def pack_kernel(pieces, which, up_ref, down_ref, up_at, down_at, out_ref):
    step = pl.program_id(0)

    @pl.when(step < pieces)
    def _():
        out_ref[...] = up_ref[0]

    @pl.when((step >= pieces) & (step < 2 * pieces))
    def _():
        out_ref[...] = down_ref[0]

    @pl.when(step == 2 * pieces)
    def _():
        ups, downs = up_at.shape[1], down_at.shape[1]
        out_ref[0:TABLE_ROWS, :] = jnp.zeros((TABLE_ROWS, out_ref.shape[1]), jnp.bfloat16)
        out_ref[0:ups, 0 : up_at.shape[2]] = up_at[0].astype(jnp.float32).astype(jnp.bfloat16)
        out_ref[ups : ups + downs, 0 : down_at.shape[2]] = (
            down_at[0].astype(jnp.float32).astype(jnp.bfloat16)
        )


def pack_weights(which, up, down, up_at, down_at):
    pieces = 2
    size, blk = up.shape[1], up.shape[2]
    step = size // pieces
    return pl.pallas_call(
        lambda *a: pack_kernel(pieces, *a),
        grid_spec=pltpu.PrefetchScalarGridSpec(
            num_scalar_prefetch=1,
            grid=(2 * pieces + 1,),
            in_specs=[
                pl.BlockSpec((1, step, blk), lambda i, w: (w[0], jnp.minimum(i, pieces - 1), 0)),
                pl.BlockSpec(
                    (1, step, blk), lambda i, w: (w[0], jnp.clip(i - pieces, 0, pieces - 1), 0)
                ),
                pl.BlockSpec((1,) + up_at.shape[1:], lambda i, w: (w[0], 0, 0)),
                pl.BlockSpec((1,) + down_at.shape[1:], lambda i, w: (w[0], 0, 0)),
            ],
            out_specs=pl.BlockSpec((step, blk), lambda i, w: (i, 0)),
        ),
        out_shape=jax.ShapeDtypeStruct((2 * size + TABLE_ROWS, blk), up.dtype),
        cost_estimate=pl.CostEstimate(flops=0, bytes_accessed=8_400_000, transcendentals=0),
        compiler_params=pltpu.CompilerParams(vmem_limit_bytes=24 * 2**20),
    )(which[None].astype(jnp.int32), up, down, up_at, down_at)


def slot_rows(first, second, experts):
    tokens = first.shape[1]
    ids = lax.broadcasted_iota(jnp.int32, (experts, tokens), 0)
    named = (ids == first) | (ids == second)
    before = lax.broadcasted_iota(jnp.int32, (tokens, tokens), 0) < lax.broadcasted_iota(
        jnp.int32, (tokens, tokens), 1
    )
    count = jnp.dot(
        jnp.where(named, 1.0, 0.0).astype(jnp.bfloat16),
        jnp.where(before, 1.0, 0.0).astype(jnp.bfloat16),
        preferred_element_type=jnp.float32,
    )
    return jnp.where(named, count.astype(jnp.int32), -1)


def gather_kernel(experts, cap, order, x_ref, choice_ref, *refs):
    outs, (slots, pick) = refs[:4], refs[4:]
    tokens = x_ref.shape[0]
    slots[...] = slot_rows(choice_ref[0, 0:1, :], choice_ref[0, 1:2, :], experts)
    row = lax.broadcasted_iota(jnp.int32, (cap, tokens), 0)
    for n in range(8):
        line = slots[pl.ds(order[n], 1), :]
        pick[n * cap : (n + 1) * cap, :] = jnp.where(line == row, 1.0, 0.0).astype(jnp.bfloat16)
    for k in range(4):
        rows = jnp.dot(
            pick[k * 2 * cap : (k + 1) * 2 * cap, :],
            x_ref[...],
            preferred_element_type=jnp.float32,
        ).astype(jnp.bfloat16)
        outs[k][0] = rows[:cap]
        outs[k][1] = rows[cap:]


def gather_rows(features, choices, order, experts, cap):
    parts, _, tokens = choices.shape
    width = features.shape[1]
    return pl.pallas_call(
        functools.partial(
            lambda *a: gather_kernel(experts, cap, *a),
        ),
        grid_spec=pltpu.PrefetchScalarGridSpec(
            num_scalar_prefetch=1,
            grid=(parts,),
            in_specs=[
                pl.BlockSpec((tokens, width), lambda b, order: (b, 0)),
                pl.BlockSpec((1, 2, tokens), lambda b, order: (b, 0, 0)),
            ],
            out_specs=[pl.BlockSpec((2, cap, width), lambda b, order: (0, b, 0))] * 4,
            scratch_shapes=[
                pltpu.VMEM((experts, tokens), jnp.int32),
                pltpu.VMEM((8 * cap, tokens), jnp.bfloat16),
            ],
        ),
        out_shape=[jax.ShapeDtypeStruct((2, parts * cap, width), jnp.bfloat16)] * 4,
        cost_estimate=pl.CostEstimate(
            flops=2 * parts * 8 * cap * tokens * width, bytes_accessed=12_000_000, transcendentals=0
        ),
        compiler_params=pltpu.CompilerParams(vmem_limit_bytes=24 * 2**20),
    )(order, features, choices)


def gelu(v):
    half = 0.5 * v
    inner = v * (math.sqrt(2 / math.pi) + (math.sqrt(2 / math.pi) * 0.044715) * (v * v))
    return half + half * jnp.tanh(inner)


def ffn_kernel(phase, n_weights, cap, meta, *refs):
    bufs, refs = refs[:8], refs[8:]
    sources, refs = refs[:n_weights], refs[n_weights:]
    outs, refs = refs[:8], refs[8:]
    xs, wts, hid, res, packed, wide, table, x_sem, w_sem, o_sem = refs
    part_rows, width = bufs[0].shape[1], bufs[0].shape[2]
    blk = wts.shape[1]
    up_cols = hid.shape[1] // blk
    down_cols = res.shape[1] // blk
    up_depth, down_depth = 2 * blk, 4 * blk
    up_size = up_cols * up_depth
    g, chosen = meta[0], meta[1]
    in_copies = []
    for n in range(8):
        col = pl.multiple_of((g ^ (n & 3)) * width, width)
        in_copies.append(
            pltpu.make_async_copy(
                bufs[n].at[phase],
                xs.at[pl.ds((n >> 2) * part_rows, part_rows), pl.ds(col, width)],
                x_sem.at[n],
            )
        )
        in_copies[-1].start()

    def weight_copies(source):
        return [
            pltpu.make_async_copy(
                source.at[pl.ds(0, up_size)], wts.at[pl.ds(0, up_size)], w_sem.at[0]
            ),
            pltpu.make_async_copy(
                source.at[pl.ds(up_size, down_cols * down_depth)],
                wts.at[pl.ds(up_size, down_cols * down_depth)],
                w_sem.at[1],
            ),
            pltpu.make_async_copy(
                source.at[pl.ds(up_size + down_cols * down_depth, TABLE_ROWS)], packed, w_sem.at[2]
            ),
        ]

    for i in range(n_weights):

        @pl.when(chosen == i)
        def _(i=i):
            for one in weight_copies(sources[i])[::-1]:
                one.start()

    weight_copies(sources[0])[2].wait()
    wide[...] = packed[...].astype(jnp.float32).astype(jnp.int32)
    to_scalars = pltpu.make_async_copy(wide, table, w_sem.at[3])
    to_scalars.start()
    for one in in_copies:
        one.wait()
    to_scalars.wait()
    weight_copies(sources[0])[0].wait()

    def up_step(col):
        parts = []
        for i in range(2):
            at = pl.multiple_of(table[col, i] * blk, blk)
            parts.append(xs[:, pl.ds(at, blk)])
        got = jnp.dot(
            jnp.concatenate(parts, axis=1),
            wts[pl.ds(pl.multiple_of(col * up_depth, up_depth), up_depth), :],
            preferred_element_type=jnp.float32,
        )
        hid[:, pl.ds(pl.multiple_of(col * blk, blk), blk)] = gelu(got).astype(jnp.bfloat16)

    def down_step(col):
        parts = []
        for i in range(4):
            at = pl.multiple_of(table[up_cols + col, i] * blk, blk)
            parts.append(hid[:, pl.ds(at, blk)])
        got = jnp.dot(
            jnp.concatenate(parts, axis=1),
            wts[pl.ds(pl.multiple_of(up_size + col * down_depth, down_depth), down_depth), :],
            preferred_element_type=jnp.float32,
        )
        res[:, pl.ds(pl.multiple_of(col * blk, blk), blk)] = got.astype(jnp.bfloat16)

    @pl.loop(0, up_cols // 2)
    def _(step):
        for i in range(2):
            up_step(step * 2 + i)

    weight_copies(sources[0])[1].wait()

    @pl.loop(0, down_cols // 2)
    def _(step):
        for i in range(2):
            down_step(step * 2 + i)

    out_copies = []
    for n in range(8):
        at = pl.multiple_of((n >> 2) * part_rows + (g ^ (n & 3)) * cap, 32)
        out_copies.append(
            pltpu.make_async_copy(res.at[pl.ds(at, cap)], outs[n], o_sem.at[n])
        )
        out_copies[-1].start()
    for one in out_copies:
        one.wait()


def expert_rows(phase, meta, bufs, weights, cap, hidden):
    _, part_rows, width = bufs[0].shape
    blk = weights[0].shape[1]
    rows, row_width = 2 * part_rows, 4 * width
    hbm = pl.BlockSpec(memory_space=pltpu.HBM)
    anywhere = pl.BlockSpec(memory_space=pl.ANY)
    smem = pl.BlockSpec(memory_space=pltpu.SMEM)
    up_and_down = weights[0].shape[0] - TABLE_ROWS
    return pl.pallas_call(
        lambda *a: ffn_kernel(phase, len(weights), cap, *a),
        in_specs=[smem] + [anywhere] * 8 + [hbm] * len(weights),
        out_specs=[anywhere] * 8,
        out_shape=[jax.ShapeDtypeStruct((cap, row_width), jnp.bfloat16)] * 8,
        scratch_shapes=[
            pltpu.VMEM((rows, row_width), jnp.bfloat16),
            pltpu.VMEM((up_and_down, blk), jnp.bfloat16),
            pltpu.VMEM((rows, hidden), jnp.bfloat16),
            pltpu.VMEM((rows, row_width), jnp.bfloat16),
            pltpu.VMEM((TABLE_ROWS, blk), jnp.bfloat16),
            pltpu.VMEM((TABLE_ROWS, blk), jnp.int32),
            pltpu.SMEM((TABLE_ROWS, blk), jnp.int32),
            pltpu.SemaphoreType.DMA((8,)),
            pltpu.SemaphoreType.DMA((4,)),
            pltpu.SemaphoreType.DMA((8,)),
        ],
        cost_estimate=pl.CostEstimate(
            flops=4 * rows * up_and_down * blk,
            bytes_accessed=12_000_000,
            transcendentals=rows * hidden,
        ),
        compiler_params=pltpu.CompilerParams(vmem_limit_bytes=40 * 2**20),
    )(meta, *bufs, *weights)


def combine_kernel(experts, cap, last, order, choice_ref, gate_ref, *refs):
    rows, refs = refs[:8], refs[8:]
    if last:
        sum_ref, refs = refs[0], refs[1:]
    out_ref, slots, high, low, stack = refs
    tokens = choice_ref.shape[1]

    @pl.when(pl.program_id(0) == 0)
    def _():
        slots[...] = slot_rows(choice_ref[0:1, :], choice_ref[1:2, :], experts)
        row = lax.broadcasted_iota(jnp.int32, (cap, tokens), 0)
        for n in range(8):
            line = slots[pl.ds(order[n], 1), :]
            gate = jnp.where(choice_ref[0:1, :] == order[n], gate_ref[0:1, :], gate_ref[1:2, :])
            top = gate.astype(jnp.bfloat16).astype(jnp.float32)
            here = line == row
            high[n * cap : (n + 1) * cap, :] = jnp.where(here, top, 0.0).astype(jnp.bfloat16)
            low[n * cap : (n + 1) * cap, :] = jnp.where(here, gate - top, 0.0).astype(jnp.bfloat16)

    for n in range(8):
        stack[n * cap : (n + 1) * cap, :] = rows[n][...]
    contract = (((0,), (0,)), ((), ()))
    total = lax.dot_general(high[...], stack[...], contract, preferred_element_type=jnp.float32)
    total += lax.dot_general(low[...], stack[...], contract, preferred_element_type=jnp.float32)
    if last:
        total += sum_ref[...]
    out_ref[...] = total.astype(out_ref.dtype)


def combine_rows(order, choice, gates, rows, so_far, experts, cap):
    tokens = choice.shape[1]
    row_width = rows[0].shape[1]
    last = so_far is not None
    chunk = 512
    block = lambda height: pl.BlockSpec((height, chunk), lambda j, order: (0, j))
    whole = pl.BlockSpec((2, tokens), lambda j, order: (0, 0))
    return pl.pallas_call(
        lambda *a: combine_kernel(experts, cap, last, *a),
        grid_spec=pltpu.PrefetchScalarGridSpec(
            num_scalar_prefetch=1,
            grid=(row_width // chunk,),
            in_specs=[whole, whole] + [block(cap)] * 8 + [block(tokens)] * last,
            out_specs=block(tokens),
            scratch_shapes=[
                pltpu.VMEM((experts, tokens), jnp.int32),
                pltpu.VMEM((8 * cap, tokens), jnp.bfloat16),
                pltpu.VMEM((8 * cap, tokens), jnp.bfloat16),
                pltpu.VMEM((8 * cap, chunk), jnp.bfloat16),
            ],
        ),
        out_shape=jax.ShapeDtypeStruct(
            (tokens, row_width), jnp.bfloat16 if last else jnp.float32
        ),
        cost_estimate=pl.CostEstimate(
            flops=4 * 8 * cap * tokens * row_width, bytes_accessed=9_000_000, transcendentals=0
        ),
        compiler_params=pltpu.CompilerParams(vmem_limit_bytes=24 * 2**20),
    )(order, choice, gates, *rows, *([so_far] if last else []))


def per_device_planes(
    attention_rows, expert_choice, gate_weights, up_blocks, up_values, down_blocks, down_values
):
    experts = 2 * lax.axis_size("exp")
    own_tokens = expert_choice.shape[1]
    cap = 3 * own_tokens // experts
    blk = up_values.shape[-1]
    hidden = up_values.shape[1] * blk
    g, at = lax.axis_index("grp"), lax.axis_index("exp")
    y, core, z, x = g // 2, g % 2, at // 2, at % 2
    features = attention_rows[0]

    own = pack_weights(
        y, up_values.reshape(2, -1, blk), down_values.reshape(2, -1, blk), up_blocks, down_blocks
    )
    r1 = send(own, along_z(1, ((0, 0), (1, 1), (2, 1))))
    l1 = send(own, along_z(-1, ((3, 0), (2, 1), (1, 1))))

    choice = expert_choice[0].T
    gates = gate_weights[0].T
    far_choice = send(choice, peer_pairs(1, 0))
    both_choices = jnp.stack([choice, far_choice])
    both_choices = lax.all_gather(after(both_choices, own), "grp", axis=1)
    far_features = send(after(features, far_choice), peer_pairs(1, 0))

    def first_second(other_x, k):
        to = g ^ k
        plane = place(to % 2, z)
        base = 2 * (x ^ other_x) + to // 2
        return 4 * plane + base, 4 * (3 - plane) + base

    order = jnp.stack([e for k in range(4) for e in first_second(0, k)]).astype(jnp.int32)

    def dispatch(rows, choices):
        parts = gather_rows(rows, choices, order, experts, cap)
        return [parts[0]] + [send(parts[k], peer_pairs(0, k)) for k in range(1, 4)]

    near = dispatch(features, both_choices[0])
    r1, l1, near, far_features = lax.optimization_barrier((r1, l1, near, far_features))
    r2 = send(r1, along_z(1, ((1, 0), (2, 1))))
    l2 = send(l1, along_z(-1, ((2, 0), (1, 1))))
    bufs = near + dispatch(far_features, both_choices[1])
    r2, l2, bufs = lax.optimization_barrier((r2, l2, bufs))
    r3 = send(r2, along_z(1, ((2, 0),)))
    l3 = send(l2, along_z(-1, ((1, 0),)))

    take_a = jnp.array([0, 2, 1, 0, 2, 0, 0, 1], jnp.int32)[z * 2 + core]
    take_b = jnp.array([5, 3, 3, 1, 2, 0, 4, 2], jnp.int32)[z * 2 + core]
    meta_a = jnp.stack([g, take_a]).astype(jnp.int32)
    meta_b = jnp.stack([g, take_b]).astype(jnp.int32)
    peers = [first_second(n >> 2, n & 3) for n in range(8)]
    order_a = jnp.stack([p[0] for p in peers]).astype(jnp.int32)
    order_b = jnp.stack([p[1] for p in peers]).astype(jnp.int32)

    def give_back(rows):
        return [rows[0]] + [send(rows[n], peer_pairs(n >> 2, n & 3)) for n in range(1, 8)]

    first = expert_rows(0, meta_a, bufs, (own, r1, l1), cap, hidden)
    back_a = give_back(first)
    r3, l3, back_a = lax.optimization_barrier((r3, l3, back_a))
    second = expert_rows(1, meta_b, bufs, (r1, l1, r2, l2, r3, l3), cap, hidden)
    back_b = give_back(second)
    sum_a = combine_rows(after(order_a, second[0]), choice, gates, back_a, None, experts, cap)
    return combine_rows(order_b, choice, gates, back_b, sum_a, experts, cap)[None]


def expert_ffn(token_rows, up_rows, up_vals, down_rows, down_vals):
    row_count, row_width = token_rows.shape
    block_size = up_vals.shape[-1]
    in_blocks = row_width // block_size
    mid_blocks = up_rows.shape[0]
    pick_up = (up_rows[:, :, None] == jnp.arange(in_blocks)[None, None, :]).astype(jnp.bfloat16)
    chosen = jnp.einsum(
        "rnb,cin->rcib",
        token_rows.reshape(row_count, in_blocks, block_size),
        pick_up,
        preferred_element_type=jnp.float32,
    ).astype(jnp.bfloat16)
    hidden = jnp.einsum("rcib,cibd->rcd", chosen, up_vals, preferred_element_type=jnp.float32)
    hidden = jax.nn.gelu(hidden, approximate=True).astype(jnp.bfloat16)
    pick_down = (down_rows[:, :, None] == jnp.arange(mid_blocks)[None, None, :]).astype(
        jnp.bfloat16
    )
    chosen_mid = jnp.einsum(
        "rcb,jic->rjib", hidden, pick_down, preferred_element_type=jnp.float32
    ).astype(jnp.bfloat16)
    result = jnp.einsum("rjib,jibd->rjd", chosen_mid, down_vals, preferred_element_type=jnp.float32)
    return result.reshape(row_count, row_width).astype(jnp.bfloat16)


def padded_rows(all_rows, weights):
    total_rows, row_width = all_rows.shape
    tile_rows = math.gcd(total_rows, 128)
    tiles = all_rows.reshape(total_rows // tile_rows, tile_rows, row_width)
    mapped = lax.map(
        lambda tile_block: expert_ffn(tile_block, weights[0], weights[1], weights[2], weights[3]),
        tiles,
    )
    return mapped.reshape(total_rows, row_width)


def slot_targets(route_ids, expert_total, capacity):
    pair_ids = route_ids.reshape(-1)
    one_hot = (pair_ids[:, None] == jnp.arange(expert_total, dtype=jnp.int32)[None, :]).astype(
        jnp.int32
    )
    earlier = jnp.cumsum(one_hot, axis=0) - one_hot
    slot_number = jnp.sum(earlier * one_hot, axis=1)
    return (pair_ids * capacity + slot_number).reshape(route_ids.shape)


def place_rows(token_rows, targets, slot_total):
    buffer_rows = jnp.zeros((slot_total, token_rows.shape[1]), token_rows.dtype)
    buffer_rows = buffer_rows.at[targets[:, 0]].set(token_rows)
    return buffer_rows.at[targets[:, 1]].set(token_rows)


def per_device(
    attention_rows, expert_choice, gate_weights, up_blocks, up_values, down_blocks, down_values
):
    group_count = lax.axis_size("grp")
    expert_devices = lax.axis_size("exp")
    local_experts = up_values.shape[0]
    expert_total = local_experts * expert_devices
    own_tokens = expert_choice.shape[1]
    capacity = 3 * own_tokens // expert_total
    head_width = attention_rows.shape[2]
    row_width = head_width * group_count
    targets = slot_targets(expert_choice[0], expert_total, capacity)
    token_rows = lax.all_to_all(attention_rows, "grp", split_axis=1, concat_axis=2, tiled=True)[0]
    send_rows = place_rows(token_rows, targets, expert_total * capacity)
    send_rows = send_rows.reshape(expert_devices, local_experts, capacity, row_width)
    received = lax.all_to_all(send_rows, "exp", split_axis=0, concat_axis=0, tiled=True)
    outputs = []
    for local_index in range(local_experts):
        weights = (
            up_blocks[local_index],
            up_values[local_index],
            down_blocks[local_index],
            down_values[local_index],
        )
        expert_rows = received[:, local_index].reshape(expert_devices * capacity, row_width)
        expert_result = padded_rows(expert_rows, weights)
        outputs.append(expert_result.reshape(expert_devices, capacity, row_width))
    stacked = jnp.stack(outputs, axis=1)
    returned = lax.all_to_all(stacked, "exp", split_axis=0, concat_axis=0, tiled=True).reshape(
        expert_total * capacity, row_width
    )
    picked = returned[targets.reshape(-1)].reshape(own_tokens, 2, row_width)
    combined = jnp.sum(gate_weights[0][:, :, None] * picked.astype(jnp.float32), axis=1)
    return combined.astype(jnp.bfloat16)[None]


def solution(mesh):
    planes = mesh.shape["grp"] == 4 and mesh.shape["exp"] == 8
    return jax.shard_map(
        per_device_planes if planes else per_device,
        mesh=mesh,
        in_specs=(
            P("exp", None, "grp"),
            P("exp", "grp", None),
            P("exp", "grp", None),
            P("exp", None, None),
            P("exp", None, None, None, None),
            P("exp", None, None),
            P("exp", None, None, None, None),
        ),
        out_specs=P("exp", "grp", None),
        check_vma=False,
    )
```

```python
import functools
import math

import jax
import jax.numpy as jnp
import numpy as np
from jax import lax
from jax.experimental import pallas as pl
from jax.experimental.pallas import tpu as pltpu
from jax.sharding import PartitionSpec as P

AXES = ("grp", "z", "x")
PLANE = ("x", "grp")


def place(core, plane):
    return jnp.where(plane < 2, core, 3 - core)


def all_pairs(rule):
    pairs = []
    for y in range(2):
        for core in range(2):
            for z in range(4):
                for x in range(2):
                    to = rule(y, core, z, x)
                    if to is not None:
                        ty, tc, tz, tx = to
                        pairs.append(((y * 2 + core) * 8 + z * 2 + x, (ty * 2 + tc) * 8 + tz * 2 + tx))
    return pairs


def along_z(step, senders):
    return all_pairs(lambda y, c, z, x: (y, c, z + step, x) if (z, c) in senders else None)


def send(value, pairs):
    return lax.ppermute(value, AXES, pairs)


def after(value, other):
    return lax.optimization_barrier((value, other))[0]


PIECES = 2
TABLE_ROWS = 16


def pack_kernel(pieces, which, up_ref, down_ref, up_at, down_at, out_ref):
    step = pl.program_id(0)

    @pl.when(step < pieces)
    def _():
        out_ref[...] = up_ref[0]

    @pl.when((step >= pieces) & (step < 2 * pieces))
    def _():
        out_ref[...] = down_ref[0]

    @pl.when(step == 2 * pieces)
    def _():
        ups, downs = up_at.shape[1], down_at.shape[1]
        out_ref[0:TABLE_ROWS, :] = jnp.zeros((TABLE_ROWS, out_ref.shape[1]), jnp.bfloat16)
        out_ref[0:ups, 0 : up_at.shape[2]] = up_at[0].astype(jnp.float32).astype(jnp.bfloat16)
        out_ref[ups : ups + downs, 0 : down_at.shape[2]] = (
            down_at[0].astype(jnp.float32).astype(jnp.bfloat16)
        )


def pack_weights(which, up, down, up_at, down_at):
    pieces = 2
    size, blk = up.shape[1], up.shape[2]
    step = size // pieces
    return pl.pallas_call(
        lambda *a: pack_kernel(pieces, *a),
        grid_spec=pltpu.PrefetchScalarGridSpec(
            num_scalar_prefetch=1,
            grid=(2 * pieces + 1,),
            in_specs=[
                pl.BlockSpec((1, step, blk), lambda i, w: (w[0], jnp.minimum(i, pieces - 1), 0)),
                pl.BlockSpec(
                    (1, step, blk), lambda i, w: (w[0], jnp.clip(i - pieces, 0, pieces - 1), 0)
                ),
                pl.BlockSpec((1,) + up_at.shape[1:], lambda i, w: (w[0], 0, 0)),
                pl.BlockSpec((1,) + down_at.shape[1:], lambda i, w: (w[0], 0, 0)),
            ],
            out_specs=pl.BlockSpec((step, blk), lambda i, w: (i, 0)),
        ),
        out_shape=jax.ShapeDtypeStruct((2 * size + TABLE_ROWS, blk), up.dtype),
        cost_estimate=pl.CostEstimate(flops=0, bytes_accessed=8_400_000, transcendentals=0),
        compiler_params=pltpu.CompilerParams(vmem_limit_bytes=60 * 2**20),
    )(which[None].astype(jnp.int32), up, down, up_at, down_at)


def slot_rows(first, second, experts):
    tokens = first.shape[1]
    ids = lax.broadcasted_iota(jnp.int32, (experts, tokens), 0)
    named = (ids == first) | (ids == second)
    before = lax.broadcasted_iota(jnp.int32, (tokens, tokens), 0) < lax.broadcasted_iota(
        jnp.int32, (tokens, tokens), 1
    )
    count = jnp.dot(
        jnp.where(named, 1.0, 0.0).astype(jnp.bfloat16),
        jnp.where(before, 1.0, 0.0).astype(jnp.bfloat16),
        preferred_element_type=jnp.float32,
    )
    return jnp.where(named, count.astype(jnp.int32), -1)


def exchange(rows):
    return lax.all_to_all(rows, PLANE, split_axis=0, concat_axis=0, tiled=True)


def gather_kernel(experts, cap, order, x_ref, choice_ref, out_ref, slots, pick):
    tokens = x_ref.shape[0]
    slots[...] = slot_rows(choice_ref[0, 0:1, :], choice_ref[0, 1:2, :], experts)
    row = lax.broadcasted_iota(jnp.int32, (cap, tokens), 0)
    for n in range(8):
        line = slots[pl.ds(order[n], 1), :]
        pick[n * cap : (n + 1) * cap, :] = jnp.where(line == row, 1.0, 0.0).astype(jnp.bfloat16)
    for n in range(0, 8, 2):
        rows = jnp.dot(
            pick[n * cap : (n + 2) * cap, :], x_ref[...], preferred_element_type=jnp.float32
        )
        out_ref[n] = rows[:cap].astype(jnp.bfloat16)
        out_ref[n + 1] = rows[cap:].astype(jnp.bfloat16)


def gather_rows(features, choices, order, experts, cap):
    parts, _, tokens = choices.shape
    width = features.shape[1]
    return pl.pallas_call(
        lambda *a: gather_kernel(experts, cap, *a),
        grid_spec=pltpu.PrefetchScalarGridSpec(
            num_scalar_prefetch=1,
            grid=(parts,),
            in_specs=[
                pl.BlockSpec((tokens, width), lambda b, order: (b, 0)),
                pl.BlockSpec((1, 2, tokens), lambda b, order: (b, 0, 0)),
            ],
            out_specs=pl.BlockSpec((8, cap, width), lambda b, order: (0, b, 0)),
            scratch_shapes=[
                pltpu.VMEM((experts, tokens), jnp.int32),
                pltpu.VMEM((8 * cap, tokens), jnp.bfloat16),
            ],
        ),
        out_shape=jax.ShapeDtypeStruct((8, parts * cap, width), jnp.bfloat16),
        cost_estimate=pl.CostEstimate(
            flops=2 * parts * 8 * cap * tokens * width, bytes_accessed=9_000_000, transcendentals=0
        ),
        compiler_params=pltpu.CompilerParams(vmem_limit_bytes=60 * 2**20),
    )(order, features, choices)


def gelu(v):
    half = 0.5 * v
    inner = v * (math.sqrt(2 / math.pi) + (math.sqrt(2 / math.pi) * 0.044715) * (v * v))
    return half + half * jnp.tanh(inner)


def ffn_kernel(n_weights, chosen, got_ref, *refs):
    sources, refs = refs[:n_weights], refs[n_weights:]
    out_ref, xs, wts, hid, res, packed, wide, table, x_sem, w_sem, o_sem = refs
    part_rows, width = got_ref.shape[1], got_ref.shape[2]
    blk = wts.shape[1]
    up_cols = hid.shape[1] // blk
    down_cols = res.shape[1] // blk
    up_depth, down_depth = 2 * blk, 4 * blk
    up_size = up_cols * up_depth

    total = up_size + down_cols * down_depth
    piece = total // PIECES

    def weight_copies(source):
        copies = [pltpu.make_async_copy(source.at[pl.ds(total, TABLE_ROWS)], packed, w_sem.at[0])]
        for n in range(PIECES):
            at = pl.ds(n * piece, piece)
            copies.append(pltpu.make_async_copy(source.at[at], wts.at[at], w_sem.at[2 + n]))
        return copies

    for i in range(n_weights):

        @pl.when(chosen[0] == i)
        def _(i=i):
            for one in weight_copies(sources[i]):
                one.start()

    in_copies = []
    for n in range(8):
        in_copies.append(
            pltpu.make_async_copy(
                got_ref.at[n],
                xs.at[
                    pl.ds((n // 4) * part_rows, part_rows), pl.ds((n % 4) * width, width)
                ],
                x_sem.at[n],
            )
        )
        in_copies[-1].start()
    waits = weight_copies(sources[0])
    waits[0].wait()
    wide[...] = packed[...].astype(jnp.float32).astype(jnp.int32)
    to_scalars = pltpu.make_async_copy(wide, table, w_sem.at[1])
    to_scalars.start()
    for one in in_copies:
        one.wait()
    to_scalars.wait()

    def block_product(source, rows, count, line, col, base):
        parts = []
        for i in range(count):
            at = pl.multiple_of(table[line + i, col] * blk, blk)
            parts.append(source[rows, pl.ds(at, blk)])
        return jnp.dot(
            jnp.concatenate(parts, axis=1),
            wts[base : base + count * blk, :],
            preferred_element_type=jnp.float32,
        )

    halves = [slice(0, part_rows), slice(part_rows, 2 * part_rows)]
    for col in range(up_cols):
        if (col * up_depth) % piece == 0:
            waits[1 + col * up_depth // piece].wait()
        for rows in halves:
            got = block_product(xs, rows, 2, 0, col, col * up_depth)
            hid[rows, col * blk : (col + 1) * blk] = gelu(got).astype(jnp.bfloat16)

    out_copies = []
    for col in range(down_cols):
        base = up_size + col * down_depth
        if base % piece == 0:
            waits[1 + base // piece].wait()
        for rows in halves:
            got = block_product(hid, rows, 4, 2, col, base)
            res[rows, col * blk : (col + 1) * blk] = got.astype(jnp.bfloat16)
        if (col + 1) % (down_cols // 2) == 0:
            half = (col + 1) // (down_cols // 2) - 1
            cols = pl.ds(half * (down_cols // 2) * blk, (down_cols // 2) * blk)
            out_copies.append(
                pltpu.make_async_copy(res.at[:, cols], out_ref.at[:, cols], o_sem.at[half])
            )
            out_copies[-1].start()
    for one in out_copies:
        one.wait()


def expert_rows(chosen, got, weights, hidden):
    _, part_rows, width = got.shape
    blk = weights[0].shape[1]
    rows, row_width = 2 * part_rows, 4 * width
    hbm = pl.BlockSpec(memory_space=pltpu.HBM)
    smem = pl.BlockSpec(memory_space=pltpu.SMEM)
    up_and_down = weights[0].shape[0] - TABLE_ROWS
    return pl.pallas_call(
        lambda *a: ffn_kernel(len(weights), *a),
        in_specs=[smem] + [hbm] * (1 + len(weights)),
        out_specs=hbm,
        out_shape=jax.ShapeDtypeStruct((rows, row_width), jnp.bfloat16),
        scratch_shapes=[
            pltpu.VMEM((rows, row_width), jnp.bfloat16),
            pltpu.VMEM((up_and_down, blk), jnp.bfloat16),
            pltpu.VMEM((rows, hidden), jnp.bfloat16),
            pltpu.VMEM((rows, row_width), jnp.bfloat16),
            pltpu.VMEM((TABLE_ROWS, blk), jnp.bfloat16),
            pltpu.VMEM((TABLE_ROWS, blk), jnp.int32),
            pltpu.SMEM((TABLE_ROWS, blk), jnp.int32),
            pltpu.SemaphoreType.DMA((8,)),
            pltpu.SemaphoreType.DMA((2 + PIECES,)),
            pltpu.SemaphoreType.DMA((2,)),
        ],
        cost_estimate=pl.CostEstimate(
            flops=4 * rows * up_and_down * blk,
            bytes_accessed=12_000_000,
            transcendentals=rows * hidden,
        ),
        compiler_params=pltpu.CompilerParams(vmem_limit_bytes=60 * 2**20),
    )(chosen[None].astype(jnp.int32), got, *weights)


def gate_matrix(order, slots, choice_ref, gate_ref, cap, high, low):
    tokens = choice_ref.shape[1]
    row = lax.broadcasted_iota(jnp.int32, (cap, tokens), 0)
    tops, rests = [], []
    for n in range(8):
        line = slots[pl.ds(order[n], 1), :]
        gate = jnp.where(choice_ref[0:1, :] == order[n], gate_ref[0:1, :], gate_ref[1:2, :])
        top = gate.astype(jnp.bfloat16).astype(jnp.float32)
        here = line == row
        tops.append(jnp.where(here, top, 0.0).astype(jnp.bfloat16))
        rests.append(jnp.where(here, gate - top, 0.0).astype(jnp.bfloat16))
    high[...] = jnp.concatenate(tops, axis=0).T
    low[...] = jnp.concatenate(rests, axis=0).T


def first_kernel(experts, cap, order_a, order_b, choice_ref, gate_ref, rows, sum_ref, *refs):
    high_b, low_b, slots, high, low = refs

    @pl.when(pl.program_id(0) == 0)
    def _():
        slots[...] = slot_rows(choice_ref[0:1, :], choice_ref[1:2, :], experts)
        gate_matrix(order_a, slots, choice_ref, gate_ref, cap, high, low)
        gate_matrix(order_b, slots, choice_ref, gate_ref, cap, high_b, low_b)

    total = jnp.dot(high[...], rows[...], preferred_element_type=jnp.float32)
    total += jnp.dot(low[...], rows[...], preferred_element_type=jnp.float32)
    sum_ref[...] = total


def combine_first(order_a, order_b, choice, gates, rows, experts, cap):
    tokens = choice.shape[1]
    columns, row_width = rows.shape
    chunk = 512
    whole = pl.BlockSpec((2, tokens), lambda j, a, c: (0, 0))
    matrix = pl.BlockSpec((tokens, columns), lambda j, a, c: (0, 0))
    return pl.pallas_call(
        lambda *a: first_kernel(experts, cap, *a),
        grid_spec=pltpu.PrefetchScalarGridSpec(
            num_scalar_prefetch=2,
            grid=(row_width // chunk,),
            in_specs=[whole, whole, pl.BlockSpec((columns, chunk), lambda j, a, c: (0, j))],
            out_specs=[pl.BlockSpec((tokens, chunk), lambda j, a, c: (0, j)), matrix, matrix],
            scratch_shapes=[
                pltpu.VMEM((experts, tokens), jnp.int32),
                pltpu.VMEM((tokens, columns), jnp.bfloat16),
                pltpu.VMEM((tokens, columns), jnp.bfloat16),
            ],
        ),
        out_shape=[jax.ShapeDtypeStruct((tokens, row_width), jnp.float32)]
        + [jax.ShapeDtypeStruct((tokens, columns), jnp.bfloat16)] * 2,
        cost_estimate=pl.CostEstimate(
            flops=4 * columns * tokens * row_width, bytes_accessed=9_000_000, transcendentals=0
        ),
        compiler_params=pltpu.CompilerParams(vmem_limit_bytes=60 * 2**20),
    )(order_a, order_b, choice, gates, rows)


def second_kernel(high, low, rows, sum_ref, out_ref):
    total = jnp.dot(high[...], rows[...], preferred_element_type=jnp.float32)
    total += jnp.dot(low[...], rows[...], preferred_element_type=jnp.float32)
    out_ref[...] = (total + sum_ref[...]).astype(out_ref.dtype)


def combine_second(high, low, rows, so_far):
    tokens, columns = high.shape
    row_width = rows.shape[1]
    chunk = 512
    matrix = pl.BlockSpec((tokens, columns), lambda j: (0, 0))
    block = pl.BlockSpec((tokens, chunk), lambda j: (0, j))
    return pl.pallas_call(
        second_kernel,
        grid=(row_width // chunk,),
        in_specs=[matrix, matrix, pl.BlockSpec((columns, chunk), lambda j: (0, j)), block],
        out_specs=block,
        out_shape=jax.ShapeDtypeStruct((tokens, row_width), jnp.bfloat16),
        cost_estimate=pl.CostEstimate(
            flops=4 * columns * tokens * row_width, bytes_accessed=9_000_000, transcendentals=0
        ),
        compiler_params=pltpu.CompilerParams(vmem_limit_bytes=60 * 2**20),
    )(high, low, rows, so_far)


def per_device_planes(
    attention_rows, expert_choice, gate_weights, up_blocks, up_values, down_blocks, down_values
):
    experts = 2 * lax.axis_size("z") * lax.axis_size("x")
    own_tokens = expert_choice.shape[1]
    cap = 3 * own_tokens // experts
    blk = up_values.shape[-1]
    hidden = up_values.shape[1] * blk
    g, z = lax.axis_index("grp"), lax.axis_index("z")
    y, core = g // 2, g % 2
    features = attention_rows[0]

    own = pack_weights(
        y,
        up_values.reshape(2, -1, blk),
        down_values.reshape(2, -1, blk),
        up_blocks.transpose(0, 2, 1),
        down_blocks.transpose(0, 2, 1),
    )
    r1 = send(own, along_z(1, ((0, 0), (1, 1), (2, 1))))
    l1 = send(own, along_z(-1, ((3, 0), (2, 1), (1, 1))))

    choice = expert_choice[0].T
    gates = gate_weights[0].T
    choices = lax.all_gather(after(choice, own), "grp")
    planes = [place(jnp.int32(d % 2), z) for d in range(8)]
    bases = [2 * (d // 4) + d % 4 // 2 for d in range(8)]
    order_a = jnp.stack([4 * planes[d] + bases[d] for d in range(8)]).astype(jnp.int32)
    order_b = jnp.stack([4 * (3 - planes[d]) + bases[d] for d in range(8)]).astype(jnp.int32)
    rows_a = gather_rows(features, choices, order_a, experts, cap)
    got_a = exchange(rows_a)
    rows_b = gather_rows(features, after(choices, rows_a), order_b, experts, cap)
    r1, l1, got_a, rows_b = lax.optimization_barrier((r1, l1, got_a, rows_b))
    r2 = send(r1, along_z(1, ((1, 0), (2, 1))))
    l2 = send(l1, along_z(-1, ((2, 0), (1, 1))))
    got_b = exchange(rows_b)

    pick = z * 2 + core
    take_a = jnp.array([0, 2, 1, 0, 2, 0, 0, 1], jnp.int32)[pick]
    take_b = jnp.array([5, 3, 3, 1, 2, 0, 4, 2], jnp.int32)[pick]
    out_a = expert_rows(take_a, got_a, (own, r1, l1), hidden)
    got_b, out_a = lax.optimization_barrier((got_b, out_a))
    back_a = exchange(out_a.reshape(8, cap, -1))
    r2, l2, out_a = lax.optimization_barrier((r2, l2, out_a))
    r3 = send(r2, along_z(1, ((2, 0),)))
    l3 = send(l2, along_z(-1, ((1, 0),)))
    r3, l3, back_a = lax.optimization_barrier((r3, l3, back_a))
    out_b = expert_rows(take_b, got_b, (r1, l1, r2, l2, r3, l3), hidden)
    back_b = exchange(out_b.reshape(8, cap, -1))
    sum_a, high, low = combine_first(
        after(order_a, out_b), order_b, choice, gates, back_a.reshape(8 * cap, -1), experts, cap
    )
    return combine_second(high, low, back_b.reshape(8 * cap, -1), sum_a)[None]


def expert_ffn(token_rows, up_rows, up_vals, down_rows, down_vals):
    row_count, row_width = token_rows.shape
    block_size = up_vals.shape[-1]
    in_blocks = row_width // block_size
    mid_blocks = up_rows.shape[0]
    pick_up = (up_rows[:, :, None] == jnp.arange(in_blocks)[None, None, :]).astype(jnp.bfloat16)
    chosen = jnp.einsum(
        "rnb,cin->rcib",
        token_rows.reshape(row_count, in_blocks, block_size),
        pick_up,
        preferred_element_type=jnp.float32,
    ).astype(jnp.bfloat16)
    hidden = jnp.einsum("rcib,cibd->rcd", chosen, up_vals, preferred_element_type=jnp.float32)
    hidden = jax.nn.gelu(hidden, approximate=True).astype(jnp.bfloat16)
    pick_down = (down_rows[:, :, None] == jnp.arange(mid_blocks)[None, None, :]).astype(
        jnp.bfloat16
    )
    chosen_mid = jnp.einsum(
        "rcb,jic->rjib", hidden, pick_down, preferred_element_type=jnp.float32
    ).astype(jnp.bfloat16)
    result = jnp.einsum("rjib,jibd->rjd", chosen_mid, down_vals, preferred_element_type=jnp.float32)
    return result.reshape(row_count, row_width).astype(jnp.bfloat16)


def padded_rows(all_rows, weights):
    total_rows, row_width = all_rows.shape
    tile_rows = math.gcd(total_rows, 128)
    tiles = all_rows.reshape(total_rows // tile_rows, tile_rows, row_width)
    mapped = lax.map(
        lambda tile_block: expert_ffn(tile_block, weights[0], weights[1], weights[2], weights[3]),
        tiles,
    )
    return mapped.reshape(total_rows, row_width)


def slot_targets(route_ids, expert_total, capacity):
    pair_ids = route_ids.reshape(-1)
    one_hot = (pair_ids[:, None] == jnp.arange(expert_total, dtype=jnp.int32)[None, :]).astype(
        jnp.int32
    )
    earlier = jnp.cumsum(one_hot, axis=0) - one_hot
    slot_number = jnp.sum(earlier * one_hot, axis=1)
    return (pair_ids * capacity + slot_number).reshape(route_ids.shape)


def place_rows(token_rows, targets, slot_total):
    buffer_rows = jnp.zeros((slot_total, token_rows.shape[1]), token_rows.dtype)
    buffer_rows = buffer_rows.at[targets[:, 0]].set(token_rows)
    return buffer_rows.at[targets[:, 1]].set(token_rows)


def per_device(
    attention_rows, expert_choice, gate_weights, up_blocks, up_values, down_blocks, down_values
):
    group_count = lax.axis_size("grp")
    expert_devices = lax.axis_size("exp")
    local_experts = up_values.shape[0]
    expert_total = local_experts * expert_devices
    own_tokens = expert_choice.shape[1]
    capacity = 3 * own_tokens // expert_total
    head_width = attention_rows.shape[2]
    row_width = head_width * group_count
    targets = slot_targets(expert_choice[0], expert_total, capacity)
    token_rows = lax.all_to_all(attention_rows, "grp", split_axis=1, concat_axis=2, tiled=True)[0]
    send_rows = place_rows(token_rows, targets, expert_total * capacity)
    send_rows = send_rows.reshape(expert_devices, local_experts, capacity, row_width)
    received = lax.all_to_all(send_rows, "exp", split_axis=0, concat_axis=0, tiled=True)
    outputs = []
    for local_index in range(local_experts):
        weights = (
            up_blocks[local_index],
            up_values[local_index],
            down_blocks[local_index],
            down_values[local_index],
        )
        expert_rows = received[:, local_index].reshape(expert_devices * capacity, row_width)
        expert_result = padded_rows(expert_rows, weights)
        outputs.append(expert_result.reshape(expert_devices, capacity, row_width))
    stacked = jnp.stack(outputs, axis=1)
    returned = lax.all_to_all(stacked, "exp", split_axis=0, concat_axis=0, tiled=True).reshape(
        expert_total * capacity, row_width
    )
    picked = returned[targets.reshape(-1)].reshape(own_tokens, 2, row_width)
    combined = jnp.sum(gate_weights[0][:, :, None] * picked.astype(jnp.float32), axis=1)
    return combined.astype(jnp.bfloat16)[None]


def solution(mesh):
    planes = mesh.shape["grp"] == 4 and mesh.shape["exp"] == 8
    exp = "exp"
    if planes:
        mesh = jax.sharding.Mesh(mesh.devices.reshape(4, 4, 2), AXES)
        exp = ("z", "x")
    return jax.shard_map(
        per_device_planes if planes else per_device,
        mesh=mesh,
        in_specs=(
            P(exp, None, "grp"),
            P(exp, "grp", None),
            P(exp, "grp", None),
            P(exp, None, None),
            P(exp, None, None, None, None),
            P(exp, None, None),
            P(exp, None, None, None, None),
        ),
        out_specs=P(exp, "grp", None),
        check_vma=False,
    )
```

```python
import functools
import math

import jax
import jax.numpy as jnp
import numpy as np
from jax import lax
from jax.experimental import pallas as pl
from jax.experimental.pallas import tpu as pltpu
from jax.sharding import PartitionSpec as P

AXES = ("grp", "z", "x")
PLANE = ("x", "grp")


def place(core, plane):
    return jnp.where(plane < 2, core, 3 - core)


def all_pairs(rule):
    pairs = []
    for y in range(2):
        for core in range(2):
            for z in range(4):
                for x in range(2):
                    to = rule(y, core, z, x)
                    if to is not None:
                        ty, tc, tz, tx = to
                        pairs.append(((y * 2 + core) * 8 + z * 2 + x, (ty * 2 + tc) * 8 + tz * 2 + tx))
    return pairs


def along_z(step, senders):
    return all_pairs(lambda y, c, z, x: (y, c, z + step, x) if (z, c) in senders else None)


def send(value, pairs):
    return lax.ppermute(value, AXES, pairs)


def after(value, other):
    return lax.optimization_barrier((value, other))[0]


PIECES = 2
TABLE_ROWS = 16


def pack_kernel(pieces, which, up_ref, down_ref, up_at, down_at, out_ref):
    step = pl.program_id(0)

    @pl.when(step < pieces)
    def _():
        out_ref[...] = up_ref[0]

    @pl.when((step >= pieces) & (step < 2 * pieces))
    def _():
        out_ref[...] = down_ref[0]

    @pl.when(step == 2 * pieces)
    def _():
        ups, downs = up_at.shape[1], down_at.shape[1]
        out_ref[0:TABLE_ROWS, :] = jnp.zeros((TABLE_ROWS, out_ref.shape[1]), jnp.bfloat16)
        out_ref[0:ups, 0 : up_at.shape[2]] = up_at[0].astype(jnp.float32).astype(jnp.bfloat16)
        out_ref[ups : ups + downs, 0 : down_at.shape[2]] = (
            down_at[0].astype(jnp.float32).astype(jnp.bfloat16)
        )


def pack_weights(which, up, down, up_at, down_at):
    pieces = 2
    size, blk = up.shape[1], up.shape[2]
    step = size // pieces
    return pl.pallas_call(
        lambda *a: pack_kernel(pieces, *a),
        grid_spec=pltpu.PrefetchScalarGridSpec(
            num_scalar_prefetch=1,
            grid=(2 * pieces + 1,),
            in_specs=[
                pl.BlockSpec((1, step, blk), lambda i, w: (w[0], jnp.minimum(i, pieces - 1), 0)),
                pl.BlockSpec(
                    (1, step, blk), lambda i, w: (w[0], jnp.clip(i - pieces, 0, pieces - 1), 0)
                ),
                pl.BlockSpec((1,) + up_at.shape[1:], lambda i, w: (w[0], 0, 0)),
                pl.BlockSpec((1,) + down_at.shape[1:], lambda i, w: (w[0], 0, 0)),
            ],
            out_specs=pl.BlockSpec((step, blk), lambda i, w: (i, 0)),
        ),
        out_shape=jax.ShapeDtypeStruct((2 * size + TABLE_ROWS, blk), up.dtype),
        cost_estimate=pl.CostEstimate(flops=0, bytes_accessed=8_400_000, transcendentals=0),
        compiler_params=pltpu.CompilerParams(vmem_limit_bytes=60 * 2**20),
    )(which[None].astype(jnp.int32), up, down, up_at, down_at)


def slot_rows(first, second, experts):
    tokens = first.shape[1]
    ids = lax.broadcasted_iota(jnp.int32, (experts, tokens), 0)
    named = (ids == first) | (ids == second)
    before = lax.broadcasted_iota(jnp.int32, (tokens, tokens), 0) < lax.broadcasted_iota(
        jnp.int32, (tokens, tokens), 1
    )
    count = jnp.dot(
        jnp.where(named, 1.0, 0.0).astype(jnp.bfloat16),
        jnp.where(before, 1.0, 0.0).astype(jnp.bfloat16),
        preferred_element_type=jnp.float32,
    )
    return jnp.where(named, count.astype(jnp.int32), -1)


def exchange(rows):
    return lax.all_to_all(rows, PLANE, split_axis=0, concat_axis=0, tiled=True)


def gather_kernel(experts, cap, order, x_ref, choice_ref, out_ref, slots, pick):
    tokens = x_ref.shape[0]
    slots[...] = slot_rows(choice_ref[0, 0:1, :], choice_ref[0, 1:2, :], experts)
    row = lax.broadcasted_iota(jnp.int32, (cap, tokens), 0)
    for n in range(8):
        line = slots[pl.ds(order[n], 1), :]
        pick[n * cap : (n + 1) * cap, :] = jnp.where(line == row, 1.0, 0.0).astype(jnp.bfloat16)
    for n in range(0, 8, 2):
        rows = jnp.dot(
            pick[n * cap : (n + 2) * cap, :], x_ref[...], preferred_element_type=jnp.float32
        )
        out_ref[n] = rows[:cap].astype(jnp.bfloat16)
        out_ref[n + 1] = rows[cap:].astype(jnp.bfloat16)


def gather_rows(features, choices, order, experts, cap):
    parts, _, tokens = choices.shape
    width = features.shape[1]
    return pl.pallas_call(
        lambda *a: gather_kernel(experts, cap, *a),
        grid_spec=pltpu.PrefetchScalarGridSpec(
            num_scalar_prefetch=1,
            grid=(parts,),
            in_specs=[
                pl.BlockSpec((tokens, width), lambda b, order: (b, 0)),
                pl.BlockSpec((1, 2, tokens), lambda b, order: (b, 0, 0)),
            ],
            out_specs=pl.BlockSpec((8, cap, width), lambda b, order: (0, b, 0)),
            scratch_shapes=[
                pltpu.VMEM((experts, tokens), jnp.int32),
                pltpu.VMEM((8 * cap, tokens), jnp.bfloat16),
            ],
        ),
        out_shape=jax.ShapeDtypeStruct((8, parts * cap, width), jnp.bfloat16),
        cost_estimate=pl.CostEstimate(
            flops=2 * parts * 8 * cap * tokens * width, bytes_accessed=9_000_000, transcendentals=0
        ),
        compiler_params=pltpu.CompilerParams(vmem_limit_bytes=60 * 2**20),
    )(order, features, choices)


def gelu(v):
    half = 0.5 * v
    inner = v * (math.sqrt(2 / math.pi) + (math.sqrt(2 / math.pi) * 0.044715) * (v * v))
    return half + half * jnp.tanh(inner)


def ffn_kernel(n_weights, chosen, got_ref, *refs):
    sources, refs = refs[:n_weights], refs[n_weights:]
    out_ref, xs, wts, hid, res, packed, wide, table, x_sem, w_sem, o_sem = refs
    part_rows, width = got_ref.shape[1], got_ref.shape[2]
    blk = wts.shape[1]
    up_cols = hid.shape[1] // blk
    down_cols = res.shape[1] // blk
    up_depth, down_depth = 2 * blk, 4 * blk
    up_size = up_cols * up_depth

    total = up_size + down_cols * down_depth
    piece = total // PIECES

    def weight_copies(source):
        copies = [pltpu.make_async_copy(source.at[pl.ds(total, TABLE_ROWS)], packed, w_sem.at[0])]
        for n in range(PIECES):
            at = pl.ds(n * piece, piece)
            copies.append(pltpu.make_async_copy(source.at[at], wts.at[at], w_sem.at[2 + n]))
        return copies

    for i in range(n_weights):

        @pl.when(chosen[0] == i)
        def _(i=i):
            for one in weight_copies(sources[i]):
                one.start()

    in_copies = []
    for n in range(8):
        in_copies.append(
            pltpu.make_async_copy(
                got_ref.at[n],
                xs.at[
                    pl.ds((n // 4) * part_rows, part_rows), pl.ds((n % 4) * width, width)
                ],
                x_sem.at[n],
            )
        )
        in_copies[-1].start()
    waits = weight_copies(sources[0])
    waits[0].wait()
    wide[...] = packed[...].astype(jnp.float32).astype(jnp.int32)
    to_scalars = pltpu.make_async_copy(wide, table, w_sem.at[1])
    to_scalars.start()
    for one in in_copies:
        one.wait()
    to_scalars.wait()

    def block_product(source, rows, count, line, col, base):
        parts = []
        for i in range(count):
            at = pl.multiple_of(table[line + i, col] * blk, blk)
            parts.append(source[rows, pl.ds(at, blk)])
        return jnp.dot(
            jnp.concatenate(parts, axis=1),
            wts[base : base + count * blk, :],
            preferred_element_type=jnp.float32,
        )

    halves = [slice(0, part_rows), slice(part_rows, 2 * part_rows)]
    for col in range(up_cols):
        if (col * up_depth) % piece == 0:
            waits[1 + col * up_depth // piece].wait()
        for rows in halves:
            got = block_product(xs, rows, 2, 0, col, col * up_depth)
            hid[rows, col * blk : (col + 1) * blk] = gelu(got).astype(jnp.bfloat16)

    out_copies = []
    for col in range(down_cols):
        base = up_size + col * down_depth
        if base % piece == 0:
            waits[1 + base // piece].wait()
        for rows in halves:
            got = block_product(hid, rows, 4, 2, col, base)
            res[rows, col * blk : (col + 1) * blk] = got.astype(jnp.bfloat16)
        if (col + 1) % (down_cols // 2) == 0:
            half = (col + 1) // (down_cols // 2) - 1
            cols = pl.ds(half * (down_cols // 2) * blk, (down_cols // 2) * blk)
            out_copies.append(
                pltpu.make_async_copy(res.at[:, cols], out_ref.at[:, cols], o_sem.at[half])
            )
            out_copies[-1].start()
    for one in out_copies:
        one.wait()


def expert_rows(chosen, got, weights, hidden):
    _, part_rows, width = got.shape
    blk = weights[0].shape[1]
    rows, row_width = 2 * part_rows, 4 * width
    hbm = pl.BlockSpec(memory_space=pltpu.HBM)
    smem = pl.BlockSpec(memory_space=pltpu.SMEM)
    up_and_down = weights[0].shape[0] - TABLE_ROWS
    return pl.pallas_call(
        lambda *a: ffn_kernel(len(weights), *a),
        in_specs=[smem] + [hbm] * (1 + len(weights)),
        out_specs=hbm,
        out_shape=jax.ShapeDtypeStruct((rows, row_width), jnp.bfloat16),
        scratch_shapes=[
            pltpu.VMEM((rows, row_width), jnp.bfloat16),
            pltpu.VMEM((up_and_down, blk), jnp.bfloat16),
            pltpu.VMEM((rows, hidden), jnp.bfloat16),
            pltpu.VMEM((rows, row_width), jnp.bfloat16),
            pltpu.VMEM((TABLE_ROWS, blk), jnp.bfloat16),
            pltpu.VMEM((TABLE_ROWS, blk), jnp.int32),
            pltpu.SMEM((TABLE_ROWS, blk), jnp.int32),
            pltpu.SemaphoreType.DMA((8,)),
            pltpu.SemaphoreType.DMA((2 + PIECES,)),
            pltpu.SemaphoreType.DMA((2,)),
        ],
        cost_estimate=pl.CostEstimate(
            flops=4 * rows * up_and_down * blk,
            bytes_accessed=12_000_000,
            transcendentals=rows * hidden,
        ),
        compiler_params=pltpu.CompilerParams(vmem_limit_bytes=60 * 2**20),
    )(chosen[None].astype(jnp.int32), got, *weights)


def gate_matrix(order, slots, choice_ref, gate_ref, cap, high, low):
    tokens = choice_ref.shape[1]
    row = lax.broadcasted_iota(jnp.int32, (cap, tokens), 0)
    tops, rests = [], []
    for n in range(8):
        line = slots[pl.ds(order[n], 1), :]
        gate = jnp.where(choice_ref[0:1, :] == order[n], gate_ref[0:1, :], gate_ref[1:2, :])
        top = gate.astype(jnp.bfloat16).astype(jnp.float32)
        here = line == row
        tops.append(jnp.where(here, top, 0.0).astype(jnp.bfloat16))
        rests.append(jnp.where(here, gate - top, 0.0).astype(jnp.bfloat16))
    high[...] = jnp.concatenate(tops, axis=0).T
    low[...] = jnp.concatenate(rests, axis=0).T


def first_kernel(experts, cap, order_a, order_b, choice_ref, gate_ref, rows, sum_ref, *refs):
    high_b, low_b, slots, high, low = refs

    @pl.when(pl.program_id(0) == 0)
    def _():
        slots[...] = slot_rows(choice_ref[0:1, :], choice_ref[1:2, :], experts)
        gate_matrix(order_a, slots, choice_ref, gate_ref, cap, high, low)
        gate_matrix(order_b, slots, choice_ref, gate_ref, cap, high_b, low_b)

    total = jnp.dot(high[...], rows[...], preferred_element_type=jnp.float32)
    total += jnp.dot(low[...], rows[...], preferred_element_type=jnp.float32)
    sum_ref[...] = total


def combine_first(order_a, order_b, choice, gates, rows, experts, cap):
    tokens = choice.shape[1]
    columns, row_width = rows.shape
    chunk = 512
    whole = pl.BlockSpec((2, tokens), lambda j, a, c: (0, 0))
    matrix = pl.BlockSpec((tokens, columns), lambda j, a, c: (0, 0))
    return pl.pallas_call(
        lambda *a: first_kernel(experts, cap, *a),
        grid_spec=pltpu.PrefetchScalarGridSpec(
            num_scalar_prefetch=2,
            grid=(row_width // chunk,),
            in_specs=[whole, whole, pl.BlockSpec((columns, chunk), lambda j, a, c: (0, j))],
            out_specs=[pl.BlockSpec((tokens, chunk), lambda j, a, c: (0, j)), matrix, matrix],
            scratch_shapes=[
                pltpu.VMEM((experts, tokens), jnp.int32),
                pltpu.VMEM((tokens, columns), jnp.bfloat16),
                pltpu.VMEM((tokens, columns), jnp.bfloat16),
            ],
        ),
        out_shape=[jax.ShapeDtypeStruct((tokens, row_width), jnp.float32)]
        + [jax.ShapeDtypeStruct((tokens, columns), jnp.bfloat16)] * 2,
        cost_estimate=pl.CostEstimate(
            flops=4 * columns * tokens * row_width, bytes_accessed=9_000_000, transcendentals=0
        ),
        compiler_params=pltpu.CompilerParams(vmem_limit_bytes=60 * 2**20),
    )(order_a, order_b, choice, gates, rows)


def second_kernel(high, low, rows, sum_ref, out_ref):
    total = jnp.dot(high[...], rows[...], preferred_element_type=jnp.float32)
    total += jnp.dot(low[...], rows[...], preferred_element_type=jnp.float32)
    out_ref[...] = (total + sum_ref[...]).astype(out_ref.dtype)


def combine_second(high, low, rows, so_far):
    tokens, columns = high.shape
    row_width = rows.shape[1]
    chunk = 512
    matrix = pl.BlockSpec((tokens, columns), lambda j: (0, 0))
    block = pl.BlockSpec((tokens, chunk), lambda j: (0, j))
    return pl.pallas_call(
        second_kernel,
        grid=(row_width // chunk,),
        in_specs=[matrix, matrix, pl.BlockSpec((columns, chunk), lambda j: (0, j)), block],
        out_specs=block,
        out_shape=jax.ShapeDtypeStruct((tokens, row_width), jnp.bfloat16),
        cost_estimate=pl.CostEstimate(
            flops=4 * columns * tokens * row_width, bytes_accessed=9_000_000, transcendentals=0
        ),
        compiler_params=pltpu.CompilerParams(vmem_limit_bytes=60 * 2**20),
    )(high, low, rows, so_far)


def per_device_planes(
    attention_rows, expert_choice, gate_weights, up_blocks, up_values, down_blocks, down_values
):
    experts = 2 * lax.axis_size("z") * lax.axis_size("x")
    own_tokens = expert_choice.shape[1]
    cap = 3 * own_tokens // experts
    blk = up_values.shape[-1]
    hidden = up_values.shape[1] * blk
    g, z = lax.axis_index("grp"), lax.axis_index("z")
    y, core = g // 2, g % 2
    features = attention_rows[0]

    own = pack_weights(
        y,
        up_values.reshape(2, -1, blk),
        down_values.reshape(2, -1, blk),
        up_blocks.transpose(0, 2, 1),
        down_blocks.transpose(0, 2, 1),
    )
    r1 = send(own, along_z(1, ((0, 0), (1, 1), (2, 1))))
    l1 = send(own, along_z(-1, ((3, 0), (2, 1), (1, 1))))

    choice = expert_choice[0].T
    gates = gate_weights[0].T
    choices = lax.all_gather(after(choice, own), "grp")
    planes = [place(jnp.int32(d % 2), z) for d in range(8)]
    bases = [2 * (d // 4) + d % 4 // 2 for d in range(8)]
    order_a = jnp.stack([4 * planes[d] + bases[d] for d in range(8)]).astype(jnp.int32)
    order_b = jnp.stack([4 * (3 - planes[d]) + bases[d] for d in range(8)]).astype(jnp.int32)
    rows_a = gather_rows(features, choices, order_a, experts, cap)
    got_a = exchange(rows_a)
    rows_b = gather_rows(features, after(choices, rows_a), order_b, experts, cap)
    r1, l1, rows_b = lax.optimization_barrier((r1, l1, rows_b))
    r2 = send(r1, along_z(1, ((1, 0), (2, 1))))
    l2 = send(l1, along_z(-1, ((2, 0), (1, 1))))
    got_a, rows_b = lax.optimization_barrier((got_a, rows_b))
    got_b = exchange(rows_b)

    pick = z * 2 + core
    take_a = jnp.array([0, 2, 1, 0, 2, 0, 0, 1], jnp.int32)[pick]
    take_b = jnp.array([5, 3, 3, 1, 2, 0, 4, 2], jnp.int32)[pick]
    out_a = expert_rows(take_a, got_a, (own, r1, l1), hidden)
    got_b, out_a = lax.optimization_barrier((got_b, out_a))
    back_a = exchange(out_a.reshape(8, cap, -1))
    r2, l2, out_a = lax.optimization_barrier((r2, l2, out_a))
    r3 = send(r2, along_z(1, ((2, 0),)))
    l3 = send(l2, along_z(-1, ((1, 0),)))
    r3, l3, back_a = lax.optimization_barrier((r3, l3, back_a))
    out_b = expert_rows(take_b, got_b, (r1, l1, r2, l2, r3, l3), hidden)
    back_b = exchange(out_b.reshape(8, cap, -1))
    sum_a, high, low = combine_first(
        after(order_a, out_b), order_b, choice, gates, back_a.reshape(8 * cap, -1), experts, cap
    )
    return combine_second(high, low, back_b.reshape(8 * cap, -1), sum_a)[None]


def expert_ffn(token_rows, up_rows, up_vals, down_rows, down_vals):
    row_count, row_width = token_rows.shape
    block_size = up_vals.shape[-1]
    in_blocks = row_width // block_size
    mid_blocks = up_rows.shape[0]
    pick_up = (up_rows[:, :, None] == jnp.arange(in_blocks)[None, None, :]).astype(jnp.bfloat16)
    chosen = jnp.einsum(
        "rnb,cin->rcib",
        token_rows.reshape(row_count, in_blocks, block_size),
        pick_up,
        preferred_element_type=jnp.float32,
    ).astype(jnp.bfloat16)
    hidden = jnp.einsum("rcib,cibd->rcd", chosen, up_vals, preferred_element_type=jnp.float32)
    hidden = jax.nn.gelu(hidden, approximate=True).astype(jnp.bfloat16)
    pick_down = (down_rows[:, :, None] == jnp.arange(mid_blocks)[None, None, :]).astype(
        jnp.bfloat16
    )
    chosen_mid = jnp.einsum(
        "rcb,jic->rjib", hidden, pick_down, preferred_element_type=jnp.float32
    ).astype(jnp.bfloat16)
    result = jnp.einsum("rjib,jibd->rjd", chosen_mid, down_vals, preferred_element_type=jnp.float32)
    return result.reshape(row_count, row_width).astype(jnp.bfloat16)


def padded_rows(all_rows, weights):
    total_rows, row_width = all_rows.shape
    tile_rows = math.gcd(total_rows, 128)
    tiles = all_rows.reshape(total_rows // tile_rows, tile_rows, row_width)
    mapped = lax.map(
        lambda tile_block: expert_ffn(tile_block, weights[0], weights[1], weights[2], weights[3]),
        tiles,
    )
    return mapped.reshape(total_rows, row_width)


def slot_targets(route_ids, expert_total, capacity):
    pair_ids = route_ids.reshape(-1)
    one_hot = (pair_ids[:, None] == jnp.arange(expert_total, dtype=jnp.int32)[None, :]).astype(
        jnp.int32
    )
    earlier = jnp.cumsum(one_hot, axis=0) - one_hot
    slot_number = jnp.sum(earlier * one_hot, axis=1)
    return (pair_ids * capacity + slot_number).reshape(route_ids.shape)


def place_rows(token_rows, targets, slot_total):
    buffer_rows = jnp.zeros((slot_total, token_rows.shape[1]), token_rows.dtype)
    buffer_rows = buffer_rows.at[targets[:, 0]].set(token_rows)
    return buffer_rows.at[targets[:, 1]].set(token_rows)


def per_device(
    attention_rows, expert_choice, gate_weights, up_blocks, up_values, down_blocks, down_values
):
    group_count = lax.axis_size("grp")
    expert_devices = lax.axis_size("exp")
    local_experts = up_values.shape[0]
    expert_total = local_experts * expert_devices
    own_tokens = expert_choice.shape[1]
    capacity = 3 * own_tokens // expert_total
    head_width = attention_rows.shape[2]
    row_width = head_width * group_count
    targets = slot_targets(expert_choice[0], expert_total, capacity)
    token_rows = lax.all_to_all(attention_rows, "grp", split_axis=1, concat_axis=2, tiled=True)[0]
    send_rows = place_rows(token_rows, targets, expert_total * capacity)
    send_rows = send_rows.reshape(expert_devices, local_experts, capacity, row_width)
    received = lax.all_to_all(send_rows, "exp", split_axis=0, concat_axis=0, tiled=True)
    outputs = []
    for local_index in range(local_experts):
        weights = (
            up_blocks[local_index],
            up_values[local_index],
            down_blocks[local_index],
            down_values[local_index],
        )
        expert_rows = received[:, local_index].reshape(expert_devices * capacity, row_width)
        expert_result = padded_rows(expert_rows, weights)
        outputs.append(expert_result.reshape(expert_devices, capacity, row_width))
    stacked = jnp.stack(outputs, axis=1)
    returned = lax.all_to_all(stacked, "exp", split_axis=0, concat_axis=0, tiled=True).reshape(
        expert_total * capacity, row_width
    )
    picked = returned[targets.reshape(-1)].reshape(own_tokens, 2, row_width)
    combined = jnp.sum(gate_weights[0][:, :, None] * picked.astype(jnp.float32), axis=1)
    return combined.astype(jnp.bfloat16)[None]


def solution(mesh):
    planes = mesh.shape["grp"] == 4 and mesh.shape["exp"] == 8
    exp = "exp"
    if planes:
        mesh = jax.sharding.Mesh(mesh.devices.reshape(4, 4, 2), AXES)
        exp = ("z", "x")
    return jax.shard_map(
        per_device_planes if planes else per_device,
        mesh=mesh,
        in_specs=(
            P(exp, None, "grp"),
            P(exp, "grp", None),
            P(exp, "grp", None),
            P(exp, None, None),
            P(exp, None, None, None, None),
            P(exp, None, None),
            P(exp, None, None, None, None),
        ),
        out_specs=P(exp, "grp", None),
        check_vma=False,
    )
```

```python
import functools
import math

import jax
import jax.numpy as jnp
import numpy as np
from jax import lax
from jax.experimental import pallas as pl
from jax.experimental.pallas import tpu as pltpu
from jax.sharding import PartitionSpec as P

AXES = ("grp", "z", "x")
PLANE = ("x", "grp")


def place(core, plane):
    return jnp.where(plane < 2, core, 3 - core)


def all_pairs(rule):
    pairs = []
    for y in range(2):
        for core in range(2):
            for z in range(4):
                for x in range(2):
                    to = rule(y, core, z, x)
                    if to is not None:
                        ty, tc, tz, tx = to
                        pairs.append(((y * 2 + core) * 8 + z * 2 + x, (ty * 2 + tc) * 8 + tz * 2 + tx))
    return pairs


def along_z(step, senders):
    return all_pairs(lambda y, c, z, x: (y, c, z + step, x) if (z, c) in senders else None)


def send(value, pairs):
    return lax.ppermute(value, AXES, pairs)


def after(value, other):
    return lax.optimization_barrier((value, other))[0]


PIECES = 2
TABLE_ROWS = 16


def pack_kernel(pieces, which, up_ref, down_ref, up_at, down_at, out_ref):
    step = pl.program_id(0)

    @pl.when(step < pieces)
    def _():
        out_ref[...] = up_ref[0]

    @pl.when((step >= pieces) & (step < 2 * pieces))
    def _():
        out_ref[...] = down_ref[0]

    @pl.when(step == 2 * pieces)
    def _():
        ups, downs = up_at.shape[1], down_at.shape[1]
        out_ref[0:TABLE_ROWS, :] = jnp.zeros((TABLE_ROWS, out_ref.shape[1]), jnp.bfloat16)
        out_ref[0:ups, 0 : up_at.shape[2]] = up_at[0].astype(jnp.float32).astype(jnp.bfloat16)
        out_ref[ups : ups + downs, 0 : down_at.shape[2]] = (
            down_at[0].astype(jnp.float32).astype(jnp.bfloat16)
        )


def pack_weights(which, up, down, up_at, down_at):
    pieces = 2
    size, blk = up.shape[1], up.shape[2]
    step = size // pieces
    return pl.pallas_call(
        lambda *a: pack_kernel(pieces, *a),
        grid_spec=pltpu.PrefetchScalarGridSpec(
            num_scalar_prefetch=1,
            grid=(2 * pieces + 1,),
            in_specs=[
                pl.BlockSpec((1, step, blk), lambda i, w: (w[0], jnp.minimum(i, pieces - 1), 0)),
                pl.BlockSpec(
                    (1, step, blk), lambda i, w: (w[0], jnp.clip(i - pieces, 0, pieces - 1), 0)
                ),
                pl.BlockSpec((1,) + up_at.shape[1:], lambda i, w: (w[0], 0, 0)),
                pl.BlockSpec((1,) + down_at.shape[1:], lambda i, w: (w[0], 0, 0)),
            ],
            out_specs=pl.BlockSpec((step, blk), lambda i, w: (i, 0)),
        ),
        out_shape=jax.ShapeDtypeStruct((2 * size + TABLE_ROWS, blk), up.dtype),
        cost_estimate=pl.CostEstimate(flops=0, bytes_accessed=8_400_000, transcendentals=0),
        compiler_params=pltpu.CompilerParams(vmem_limit_bytes=60 * 2**20),
    )(which[None].astype(jnp.int32), up, down, up_at, down_at)


def slot_rows(first, second, experts):
    tokens = first.shape[1]
    ids = lax.broadcasted_iota(jnp.int32, (experts, tokens), 0)
    named = (ids == first) | (ids == second)
    before = lax.broadcasted_iota(jnp.int32, (tokens, tokens), 0) < lax.broadcasted_iota(
        jnp.int32, (tokens, tokens), 1
    )
    count = jnp.dot(
        jnp.where(named, 1.0, 0.0).astype(jnp.bfloat16),
        jnp.where(before, 1.0, 0.0).astype(jnp.bfloat16),
        preferred_element_type=jnp.float32,
    )
    return jnp.where(named, count.astype(jnp.int32), -1)


def exchange(rows):
    return lax.all_to_all(rows, PLANE, split_axis=0, concat_axis=0, tiled=True)


def gather_kernel(experts, cap, order, x_ref, choice_ref, out_ref, slots, pick):
    tokens = x_ref.shape[0]
    slots[...] = slot_rows(choice_ref[0, 0:1, :], choice_ref[0, 1:2, :], experts)
    row = lax.broadcasted_iota(jnp.int32, (cap, tokens), 0)
    for n in range(8):
        line = slots[pl.ds(order[n], 1), :]
        pick[n * cap : (n + 1) * cap, :] = jnp.where(line == row, 1.0, 0.0).astype(jnp.bfloat16)
    for n in range(0, 8, 2):
        rows = jnp.dot(
            pick[n * cap : (n + 2) * cap, :], x_ref[...], preferred_element_type=jnp.float32
        )
        out_ref[n] = rows[:cap].astype(jnp.bfloat16)
        out_ref[n + 1] = rows[cap:].astype(jnp.bfloat16)


def gather_rows(features, choices, order, experts, cap):
    parts, _, tokens = choices.shape
    width = features.shape[1]
    return pl.pallas_call(
        lambda *a: gather_kernel(experts, cap, *a),
        grid_spec=pltpu.PrefetchScalarGridSpec(
            num_scalar_prefetch=1,
            grid=(parts,),
            in_specs=[
                pl.BlockSpec((tokens, width), lambda b, order: (b, 0)),
                pl.BlockSpec((1, 2, tokens), lambda b, order: (b, 0, 0)),
            ],
            out_specs=pl.BlockSpec((8, cap, width), lambda b, order: (0, b, 0)),
            scratch_shapes=[
                pltpu.VMEM((experts, tokens), jnp.int32),
                pltpu.VMEM((8 * cap, tokens), jnp.bfloat16),
            ],
        ),
        out_shape=jax.ShapeDtypeStruct((8, parts * cap, width), jnp.bfloat16),
        cost_estimate=pl.CostEstimate(
            flops=2 * parts * 8 * cap * tokens * width, bytes_accessed=9_000_000, transcendentals=0
        ),
        compiler_params=pltpu.CompilerParams(vmem_limit_bytes=60 * 2**20),
    )(order, features, choices)


def gelu(v):
    half = 0.5 * v
    inner = v * (math.sqrt(2 / math.pi) + (math.sqrt(2 / math.pi) * 0.044715) * (v * v))
    return half + half * jnp.tanh(inner)


def ffn_kernel(n_weights, cap, meta, *refs):
    @pl.when(meta[1] == 1)
    def _():
        run_expert(n_weights, cap, meta[0], *refs)


def run_expert(n_weights, cap, chosen, got_ref, *refs):
    sources, refs = refs[:n_weights], refs[n_weights:]
    outs, refs = refs[:-10], refs[-10:]
    xs, wts, hid, res, packed, wide, table, x_sem, w_sem, o_sem = refs
    part_rows, width = got_ref.shape[1], got_ref.shape[2]
    blk = wts.shape[1]
    up_cols = hid.shape[1] // blk
    down_cols = res.shape[1] // blk
    up_depth, down_depth = 2 * blk, 4 * blk
    up_size = up_cols * up_depth

    total = up_size + down_cols * down_depth
    piece = total // PIECES

    def weight_copies(source):
        copies = [pltpu.make_async_copy(source.at[pl.ds(total, TABLE_ROWS)], packed, w_sem.at[0])]
        for n in range(PIECES):
            at = pl.ds(n * piece, piece)
            copies.append(pltpu.make_async_copy(source.at[at], wts.at[at], w_sem.at[2 + n]))
        return copies

    for i in range(n_weights):

        @pl.when(chosen == i)
        def _(i=i):
            for one in weight_copies(sources[i]):
                one.start()

    in_copies = []
    for n in range(8):
        in_copies.append(
            pltpu.make_async_copy(
                got_ref.at[n],
                xs.at[
                    pl.ds((n // 4) * part_rows, part_rows), pl.ds((n % 4) * width, width)
                ],
                x_sem.at[n],
            )
        )
        in_copies[-1].start()
    waits = weight_copies(sources[0])
    waits[0].wait()
    wide[...] = packed[...].astype(jnp.float32).astype(jnp.int32)
    to_scalars = pltpu.make_async_copy(wide, table, w_sem.at[1])
    to_scalars.start()
    for one in in_copies:
        one.wait()
    to_scalars.wait()

    def block_product(source, rows, count, line, col, base):
        parts = []
        for i in range(count):
            at = pl.multiple_of(table[line + i, col] * blk, blk)
            parts.append(source[rows, pl.ds(at, blk)])
        return jnp.dot(
            jnp.concatenate(parts, axis=1),
            wts[base : base + count * blk, :],
            preferred_element_type=jnp.float32,
        )

    halves = [slice(0, part_rows), slice(part_rows, 2 * part_rows)]
    for col in range(up_cols):
        if (col * up_depth) % piece == 0:
            waits[1 + col * up_depth // piece].wait()
        for rows in halves:
            got = block_product(xs, rows, 2, 0, col, col * up_depth)
            hid[rows, col * blk : (col + 1) * blk] = gelu(got).astype(jnp.bfloat16)

    out_copies = []
    for col in range(down_cols):
        base = up_size + col * down_depth
        if base % piece == 0:
            waits[1 + base // piece].wait()
        for rows in halves:
            got = block_product(hid, rows, 4, 2, col, base)
            res[rows, col * blk : (col + 1) * blk] = got.astype(jnp.bfloat16)
        if (col + 1) % (down_cols // 2) == 0:
            half = (col + 1) // (down_cols // 2) - 1
            cols = pl.ds(half * (down_cols // 2) * blk, (down_cols // 2) * blk)
            share = cap // len(outs)
            for n in range(8 * len(outs)):
                owner, part = n // len(outs), n % len(outs)
                out_copies.append(
                    pltpu.make_async_copy(
                        res.at[pl.ds(owner * cap + part * share, share), cols],
                        outs[part].at[pl.ds(owner * share, share), cols],
                        o_sem.at[half * 8 * len(outs) + n],
                    )
                )
                out_copies[-1].start()
    for one in out_copies:
        one.wait()


def expert_rows(chosen, active, got, weights, hidden, cap, shares):
    _, part_rows, width = got.shape
    blk = weights[0].shape[1]
    rows, row_width = 2 * part_rows, 4 * width
    hbm = pl.BlockSpec(memory_space=pltpu.HBM)
    smem = pl.BlockSpec(memory_space=pltpu.SMEM)
    up_and_down = weights[0].shape[0] - TABLE_ROWS
    return pl.pallas_call(
        lambda *a: ffn_kernel(len(weights), cap, *a),
        in_specs=[smem] + [hbm] * (1 + len(weights)),
        out_specs=[hbm] * shares,
        out_shape=[jax.ShapeDtypeStruct((rows // shares, row_width), jnp.bfloat16)] * shares,
        scratch_shapes=[
            pltpu.VMEM((rows, row_width), jnp.bfloat16),
            pltpu.VMEM((up_and_down, blk), jnp.bfloat16),
            pltpu.VMEM((rows, hidden), jnp.bfloat16),
            pltpu.VMEM((rows, row_width), jnp.bfloat16),
            pltpu.VMEM((TABLE_ROWS, blk), jnp.bfloat16),
            pltpu.VMEM((TABLE_ROWS, blk), jnp.int32),
            pltpu.SMEM((TABLE_ROWS, blk), jnp.int32),
            pltpu.SemaphoreType.DMA((8,)),
            pltpu.SemaphoreType.DMA((2 + PIECES,)),
            pltpu.SemaphoreType.DMA((32,)),
        ],
        cost_estimate=pl.CostEstimate(
            flops=4 * rows * up_and_down * blk,
            bytes_accessed=12_000_000,
            transcendentals=rows * hidden,
        ),
        compiler_params=pltpu.CompilerParams(vmem_limit_bytes=60 * 2**20),
    )(jnp.stack([chosen, active]).astype(jnp.int32), got, *weights)


def gate_matrix(order, blocks, slots, choice_ref, gate_ref, high, low):
    tokens = choice_ref.shape[1]
    tops, rests = [], []
    for n, size, first in blocks:
        row = lax.broadcasted_iota(jnp.int32, (size, tokens), 0) + first
        line = slots[pl.ds(order[n], 1), :]
        gate = jnp.where(choice_ref[0:1, :] == order[n], gate_ref[0:1, :], gate_ref[1:2, :])
        top = gate.astype(jnp.bfloat16).astype(jnp.float32)
        here = line == row
        tops.append(jnp.where(here, top, 0.0).astype(jnp.bfloat16))
        rests.append(jnp.where(here, gate - top, 0.0).astype(jnp.bfloat16))
    high[...] = jnp.concatenate(tops, axis=0).T
    low[...] = jnp.concatenate(rests, axis=0).T


def first_kernel(experts, cap, order, choice_ref, gate_ref, rows_a, rows_1, sum_ref, *refs):
    high_b, low_b, slots, high, low, stack = refs
    part = cap // 2

    def of_core(on):
        return [(8 + 8 * (1 - on) + s, part, part * ((s % 2) ^ on)) for s in range(8)]

    @pl.when(pl.program_id(0) == 0)
    def _():
        slots[...] = slot_rows(choice_ref[0:1, :], choice_ref[1:2, :], experts)
        blocks = [(n, cap, 0) for n in range(8)] + of_core(1)
        gate_matrix(order, blocks, slots, choice_ref, gate_ref, high, low)
        gate_matrix(order, of_core(0), slots, choice_ref, gate_ref, high_b, low_b)

    stack[0 : 8 * cap, :] = rows_a[...]
    stack[8 * cap :, :] = rows_1[...]
    total = jnp.dot(high[...], stack[...], preferred_element_type=jnp.float32)
    total += jnp.dot(low[...], stack[...], preferred_element_type=jnp.float32)
    sum_ref[...] = total


def combine_first(order, choice, gates, rows_a, rows_1, experts, cap):
    tokens = choice.shape[1]
    row_width = rows_a.shape[1]
    count_a, count_1 = rows_a.shape[0], rows_1.shape[0]
    chunk = 512
    whole = pl.BlockSpec((2, tokens), lambda j, a: (0, 0))
    matrix = pl.BlockSpec((tokens, count_1), lambda j, a: (0, 0))
    return pl.pallas_call(
        lambda *a: first_kernel(experts, cap, *a),
        grid_spec=pltpu.PrefetchScalarGridSpec(
            num_scalar_prefetch=1,
            grid=(row_width // chunk,),
            in_specs=[
                whole,
                whole,
                pl.BlockSpec((count_a, chunk), lambda j, a: (0, j)),
                pl.BlockSpec((count_1, chunk), lambda j, a: (0, j)),
            ],
            out_specs=[pl.BlockSpec((tokens, chunk), lambda j, a: (0, j)), matrix, matrix],
            scratch_shapes=[
                pltpu.VMEM((experts, tokens), jnp.int32),
                pltpu.VMEM((tokens, count_a + count_1), jnp.bfloat16),
                pltpu.VMEM((tokens, count_a + count_1), jnp.bfloat16),
                pltpu.VMEM((count_a + count_1, chunk), jnp.bfloat16),
            ],
        ),
        out_shape=[jax.ShapeDtypeStruct((tokens, row_width), jnp.float32)]
        + [jax.ShapeDtypeStruct((tokens, count_1), jnp.bfloat16)] * 2,
        cost_estimate=pl.CostEstimate(
            flops=4 * (count_a + count_1) * tokens * row_width,
            bytes_accessed=9_000_000,
            transcendentals=0,
        ),
        compiler_params=pltpu.CompilerParams(vmem_limit_bytes=60 * 2**20),
    )(order, choice, gates, rows_a, rows_1)


def second_kernel(high, low, rows, sum_ref, out_ref):
    total = jnp.dot(high[...], rows[...], preferred_element_type=jnp.float32)
    total += jnp.dot(low[...], rows[...], preferred_element_type=jnp.float32)
    out_ref[...] = (total + sum_ref[...]).astype(out_ref.dtype)


def combine_second(high, low, rows, so_far):
    tokens, columns = high.shape
    row_width = rows.shape[1]
    chunk = 512
    matrix = pl.BlockSpec((tokens, columns), lambda j: (0, 0))
    block = pl.BlockSpec((tokens, chunk), lambda j: (0, j))
    return pl.pallas_call(
        second_kernel,
        grid=(row_width // chunk,),
        in_specs=[matrix, matrix, pl.BlockSpec((columns, chunk), lambda j: (0, j)), block],
        out_specs=block,
        out_shape=jax.ShapeDtypeStruct((tokens, row_width), jnp.bfloat16),
        cost_estimate=pl.CostEstimate(
            flops=4 * columns * tokens * row_width, bytes_accessed=9_000_000, transcendentals=0
        ),
        compiler_params=pltpu.CompilerParams(vmem_limit_bytes=60 * 2**20),
    )(high, low, rows, so_far)


def per_device_planes(
    attention_rows, expert_choice, gate_weights, up_blocks, up_values, down_blocks, down_values
):
    experts = 2 * lax.axis_size("z") * lax.axis_size("x")
    own_tokens = expert_choice.shape[1]
    cap = 3 * own_tokens // experts
    blk = up_values.shape[-1]
    hidden = up_values.shape[1] * blk
    g, z = lax.axis_index("grp"), lax.axis_index("z")
    y, core = g // 2, g % 2
    features = attention_rows[0]

    own = pack_weights(
        y,
        up_values.reshape(2, -1, blk),
        down_values.reshape(2, -1, blk),
        up_blocks.transpose(0, 2, 1),
        down_blocks.transpose(0, 2, 1),
    )
    r1 = send(own, along_z(1, ((0, 0), (1, 1), (2, 1))))
    l1 = send(own, along_z(-1, ((3, 0), (2, 1), (1, 1))))

    choice = expert_choice[0].T
    gates = gate_weights[0].T
    choices = lax.all_gather(after(choice, own), "grp")
    planes = [place(jnp.int32(d % 2), z) for d in range(8)]
    bases = [2 * (d // 4) + d % 4 // 2 for d in range(8)]
    order_a = jnp.stack([4 * planes[d] + bases[d] for d in range(8)]).astype(jnp.int32)
    order_b = jnp.stack([4 * (3 - planes[d]) + bases[d] for d in range(8)]).astype(jnp.int32)
    rows_a = gather_rows(features, choices, order_a, experts, cap)
    got_a = exchange(rows_a)
    rows_b = gather_rows(features, after(choices, rows_a), order_b, experts, cap)
    r1, l1, rows_b = lax.optimization_barrier((r1, l1, rows_b))
    r2 = send(r1, along_z(1, ((1, 0), (2, 1))))
    l2 = send(l1, along_z(-1, ((2, 0), (1, 1))))
    got_a, rows_b = lax.optimization_barrier((got_a, rows_b))
    got_b = exchange(rows_b)

    pick = z * 2 + core
    take_a = jnp.array([0, 2, 1, 0, 2, 0, 0, 1], jnp.int32)[pick]
    (out_a,) = expert_rows(take_a, jnp.int32(1), got_a, (own, r1, l1), hidden, cap, 1)
    got_b, out_a = lax.optimization_barrier((got_b, out_a))
    back_a = exchange(out_a.reshape(8, cap, -1)).reshape(8 * cap, -1)
    r2, l2, out_a = lax.optimization_barrier((r2, l2, out_a))
    r3 = send(r2, along_z(1, ((2, 0),)))
    l3 = send(l2, along_z(-1, ((1, 0),)))

    def second(on, chosen, weights, earlier):
        keep, give = expert_rows(chosen[pick], core == on, got_b, weights, hidden, cap, 2)
        earlier, keep, give = lax.optimization_barrier((earlier, keep, give))
        taken = send(give, all_pairs(lambda y, c, z, x: (y, 1 - c, z, x) if c == on else None))
        return jnp.where(core == on, keep, taken), earlier

    def give_back(rows):
        return exchange(rows.reshape(8, cap // 2, -1)).reshape(4 * cap, -1)

    rows_1, _ = second(1, jnp.array([0, 3, 0, 1, 0, 2, 0, 0], jnp.int32), (r2, l1, r1, l2), ())
    back_a, rows_1 = lax.optimization_barrier((back_a, rows_1))
    back_1 = give_back(rows_1)
    r3, l3, got_b = lax.optimization_barrier((r3, l3, after(got_b, rows_1)))
    rows_0, back_1 = second(
        0, jnp.array([3, 0, 2, 0, 1, 0, 0, 0], jnp.int32), (r3, r2, l2, l3), back_1
    )
    back_0 = give_back(rows_0)
    order_c = [
        4 * (3 - place(jnp.int32(on), z)) + 2 * (s // 4) + s % 4 // 2
        for on in (1, 0)
        for s in range(8)
    ]
    order = jnp.concatenate([order_a, jnp.stack(order_c).astype(jnp.int32)])
    sum_a, high, low = combine_first(
        after(order, rows_0), choice, gates, back_a, back_1, experts, cap
    )
    return combine_second(high, low, back_0, sum_a)[None]


def expert_ffn(token_rows, up_rows, up_vals, down_rows, down_vals):
    row_count, row_width = token_rows.shape
    block_size = up_vals.shape[-1]
    in_blocks = row_width // block_size
    mid_blocks = up_rows.shape[0]
    pick_up = (up_rows[:, :, None] == jnp.arange(in_blocks)[None, None, :]).astype(jnp.bfloat16)
    chosen = jnp.einsum(
        "rnb,cin->rcib",
        token_rows.reshape(row_count, in_blocks, block_size),
        pick_up,
        preferred_element_type=jnp.float32,
    ).astype(jnp.bfloat16)
    hidden = jnp.einsum("rcib,cibd->rcd", chosen, up_vals, preferred_element_type=jnp.float32)
    hidden = jax.nn.gelu(hidden, approximate=True).astype(jnp.bfloat16)
    pick_down = (down_rows[:, :, None] == jnp.arange(mid_blocks)[None, None, :]).astype(
        jnp.bfloat16
    )
    chosen_mid = jnp.einsum(
        "rcb,jic->rjib", hidden, pick_down, preferred_element_type=jnp.float32
    ).astype(jnp.bfloat16)
    result = jnp.einsum("rjib,jibd->rjd", chosen_mid, down_vals, preferred_element_type=jnp.float32)
    return result.reshape(row_count, row_width).astype(jnp.bfloat16)


def padded_rows(all_rows, weights):
    total_rows, row_width = all_rows.shape
    tile_rows = math.gcd(total_rows, 128)
    tiles = all_rows.reshape(total_rows // tile_rows, tile_rows, row_width)
    mapped = lax.map(
        lambda tile_block: expert_ffn(tile_block, weights[0], weights[1], weights[2], weights[3]),
        tiles,
    )
    return mapped.reshape(total_rows, row_width)


def slot_targets(route_ids, expert_total, capacity):
    pair_ids = route_ids.reshape(-1)
    one_hot = (pair_ids[:, None] == jnp.arange(expert_total, dtype=jnp.int32)[None, :]).astype(
        jnp.int32
    )
    earlier = jnp.cumsum(one_hot, axis=0) - one_hot
    slot_number = jnp.sum(earlier * one_hot, axis=1)
    return (pair_ids * capacity + slot_number).reshape(route_ids.shape)


def place_rows(token_rows, targets, slot_total):
    buffer_rows = jnp.zeros((slot_total, token_rows.shape[1]), token_rows.dtype)
    buffer_rows = buffer_rows.at[targets[:, 0]].set(token_rows)
    return buffer_rows.at[targets[:, 1]].set(token_rows)


def per_device(
    attention_rows, expert_choice, gate_weights, up_blocks, up_values, down_blocks, down_values
):
    group_count = lax.axis_size("grp")
    expert_devices = lax.axis_size("exp")
    local_experts = up_values.shape[0]
    expert_total = local_experts * expert_devices
    own_tokens = expert_choice.shape[1]
    capacity = 3 * own_tokens // expert_total
    head_width = attention_rows.shape[2]
    row_width = head_width * group_count
    targets = slot_targets(expert_choice[0], expert_total, capacity)
    token_rows = lax.all_to_all(attention_rows, "grp", split_axis=1, concat_axis=2, tiled=True)[0]
    send_rows = place_rows(token_rows, targets, expert_total * capacity)
    send_rows = send_rows.reshape(expert_devices, local_experts, capacity, row_width)
    received = lax.all_to_all(send_rows, "exp", split_axis=0, concat_axis=0, tiled=True)
    outputs = []
    for local_index in range(local_experts):
        weights = (
            up_blocks[local_index],
            up_values[local_index],
            down_blocks[local_index],
            down_values[local_index],
        )
        expert_rows = received[:, local_index].reshape(expert_devices * capacity, row_width)
        expert_result = padded_rows(expert_rows, weights)
        outputs.append(expert_result.reshape(expert_devices, capacity, row_width))
    stacked = jnp.stack(outputs, axis=1)
    returned = lax.all_to_all(stacked, "exp", split_axis=0, concat_axis=0, tiled=True).reshape(
        expert_total * capacity, row_width
    )
    picked = returned[targets.reshape(-1)].reshape(own_tokens, 2, row_width)
    combined = jnp.sum(gate_weights[0][:, :, None] * picked.astype(jnp.float32), axis=1)
    return combined.astype(jnp.bfloat16)[None]


def solution(mesh):
    planes = mesh.shape["grp"] == 4 and mesh.shape["exp"] == 8
    exp = "exp"
    if planes:
        mesh = jax.sharding.Mesh(mesh.devices.reshape(4, 4, 2), AXES)
        exp = ("z", "x")
    return jax.shard_map(
        per_device_planes if planes else per_device,
        mesh=mesh,
        in_specs=(
            P(exp, None, "grp"),
            P(exp, "grp", None),
            P(exp, "grp", None),
            P(exp, None, None),
            P(exp, None, None, None, None),
            P(exp, None, None),
            P(exp, None, None, None, None),
        ),
        out_specs=P(exp, "grp", None),
        check_vma=False,
    )
```

```python
import functools
import math

import jax
import jax.numpy as jnp
import numpy as np
from jax import lax
from jax.experimental import pallas as pl
from jax.experimental.pallas import tpu as pltpu
from jax.sharding import PartitionSpec as P

AXES = ("grp", "z", "x")
PLANE = ("x", "grp")


def place(core, plane):
    return jnp.where(plane < 2, core, 3 - core)


def all_pairs(rule):
    pairs = []
    for y in range(2):
        for core in range(2):
            for z in range(4):
                for x in range(2):
                    to = rule(y, core, z, x)
                    if to is not None:
                        ty, tc, tz, tx = to
                        pairs.append(((y * 2 + core) * 8 + z * 2 + x, (ty * 2 + tc) * 8 + tz * 2 + tx))
    return pairs


def along_z(step, senders):
    return all_pairs(lambda y, c, z, x: (y, c, z + step, x) if (z, c) in senders else None)


def send(value, pairs):
    return lax.ppermute(value, AXES, pairs)


def after(value, other):
    return lax.optimization_barrier((value, other))[0]


PIECES = 2
TABLE_ROWS = 16


def pack_kernel(pieces, which, up, down, up_at, down_at, out, held, rows, in_sem, out_sem):
    size = up.shape[1]
    step = size // pieces
    inward, outward = [], []
    for n in range(2 * pieces):
        source, at = (up, n * step) if n < pieces else (down, (n - pieces) * step)
        here = held.at[pl.ds(n * step, step)]
        inward.append(
            pltpu.make_async_copy(source.at[which[0], pl.ds(at, step)], here, in_sem.at[n])
        )
        outward.append(
            pltpu.make_async_copy(here, out.at[pl.ds(n * step, step)], out_sem.at[n])
        )
        inward[-1].start()
    ups, downs = up_at.shape[1], down_at.shape[1]
    rows[...] = jnp.zeros(rows.shape, jnp.bfloat16)
    rows[0:ups, 0 : up_at.shape[2]] = up_at[which[0]].astype(jnp.float32).astype(jnp.bfloat16)
    rows[ups : ups + downs, 0 : down_at.shape[2]] = (
        down_at[which[0]].astype(jnp.float32).astype(jnp.bfloat16)
    )
    outward.append(
        pltpu.make_async_copy(rows, out.at[pl.ds(2 * size, TABLE_ROWS)], out_sem.at[2 * pieces])
    )
    outward[-1].start()
    for n in range(2 * pieces):
        inward[n].wait()
        outward[n].start()
    for one in outward:
        one.wait()


def pack_weights(which, up, down, up_at, down_at):
    pieces = 4
    size, blk = up.shape[1], up.shape[2]
    hbm = pl.BlockSpec(memory_space=pltpu.HBM)
    vmem = pl.BlockSpec(memory_space=pltpu.VMEM)
    return pl.pallas_call(
        lambda *a: pack_kernel(pieces, *a),
        in_specs=[pl.BlockSpec(memory_space=pltpu.SMEM), hbm, hbm, vmem, vmem],
        out_specs=hbm,
        out_shape=jax.ShapeDtypeStruct((2 * size + TABLE_ROWS, blk), up.dtype),
        scratch_shapes=[
            pltpu.VMEM((2 * size, blk), jnp.bfloat16),
            pltpu.VMEM((TABLE_ROWS, blk), jnp.bfloat16),
            pltpu.SemaphoreType.DMA((2 * pieces,)),
            pltpu.SemaphoreType.DMA((2 * pieces + 1,)),
        ],
        cost_estimate=pl.CostEstimate(flops=0, bytes_accessed=8_400_000, transcendentals=0),
        compiler_params=pltpu.CompilerParams(vmem_limit_bytes=60 * 2**20),
    )(which[None].astype(jnp.int32), up, down, up_at, down_at)


def slot_rows(pairs, experts):
    tokens = pairs[0][0].shape[1]
    ids = lax.broadcasted_iota(jnp.int32, (experts, tokens), 0)
    named = [jnp.where((ids == a) | (ids == b), 1.0, 0.0) for a, b in pairs]
    named = jnp.concatenate(named, axis=0)
    before = lax.broadcasted_iota(jnp.int32, (tokens, tokens), 0) < lax.broadcasted_iota(
        jnp.int32, (tokens, tokens), 1
    )
    count = jnp.dot(
        named.astype(jnp.bfloat16),
        jnp.where(before, 1.0, 0.0).astype(jnp.bfloat16),
        preferred_element_type=jnp.float32,
    )
    return jnp.where(named > 0.5, count.astype(jnp.int32), -1)


def exchange(rows):
    return lax.all_to_all(rows, PLANE, split_axis=0, concat_axis=0, tiled=True)


def gather_kernel(experts, cap, order, x_ref, choice_ref, out_ref, slots, pick):
    tokens = x_ref.shape[0]
    part = pl.program_id(0)

    @pl.when(part == 0)
    def _():
        pairs = [(choice_ref[b, 0:1, :], choice_ref[b, 1:2, :]) for b in range(choice_ref.shape[0])]
        slots[...] = slot_rows(pairs, experts)

    row = lax.broadcasted_iota(jnp.int32, (cap, tokens), 0)
    for n in range(8):
        line = slots[pl.ds(part * experts + order[n], 1), :]
        pick[n * cap : (n + 1) * cap, :] = jnp.where(line == row, 1.0, 0.0).astype(jnp.bfloat16)
    for n in range(0, 8, 2):
        rows = jnp.dot(
            pick[n * cap : (n + 2) * cap, :], x_ref[...], preferred_element_type=jnp.float32
        )
        out_ref[n] = rows[:cap].astype(jnp.bfloat16)
        out_ref[n + 1] = rows[cap:].astype(jnp.bfloat16)


def gather_rows(features, choices, order, experts, cap):
    parts, _, tokens = choices.shape
    width = features.shape[1]
    return pl.pallas_call(
        lambda *a: gather_kernel(experts, cap, *a),
        grid_spec=pltpu.PrefetchScalarGridSpec(
            num_scalar_prefetch=1,
            grid=(parts,),
            in_specs=[
                pl.BlockSpec((tokens, width), lambda b, order: (b, 0)),
                pl.BlockSpec((parts, 2, tokens), lambda b, order: (0, 0, 0)),
            ],
            out_specs=pl.BlockSpec((8, cap, width), lambda b, order: (0, b, 0)),
            scratch_shapes=[
                pltpu.VMEM((parts * experts, tokens), jnp.int32),
                pltpu.VMEM((8 * cap, tokens), jnp.bfloat16),
            ],
        ),
        out_shape=jax.ShapeDtypeStruct((8, parts * cap, width), jnp.bfloat16),
        cost_estimate=pl.CostEstimate(
            flops=2 * parts * 8 * cap * tokens * width, bytes_accessed=9_000_000, transcendentals=0
        ),
        compiler_params=pltpu.CompilerParams(vmem_limit_bytes=60 * 2**20),
    )(order, features, choices)


def gelu(v):
    half = 0.5 * v
    inner = v * (math.sqrt(2 / math.pi) + (math.sqrt(2 / math.pi) * 0.044715) * (v * v))
    return half + half * jnp.tanh(inner)


def ffn_kernel(n_weights, cap, meta, *refs):
    @pl.when(meta[1] == 1)
    def _():
        run_expert(n_weights, cap, meta[0], *refs)


def run_expert(n_weights, cap, chosen, got_ref, *refs):
    sources, refs = refs[:n_weights], refs[n_weights:]
    outs, refs = refs[:-10], refs[-10:]
    xs, wts, hid, res, packed, wide, table, x_sem, w_sem, o_sem = refs
    part_rows, width = got_ref.shape[1], got_ref.shape[2]
    blk = wts.shape[1]
    up_cols = hid.shape[1] // blk
    down_cols = res.shape[1] // blk
    up_depth, down_depth = 2 * blk, 4 * blk
    up_size = up_cols * up_depth

    total = up_size + down_cols * down_depth
    piece = total // PIECES

    def weight_copies(source):
        copies = [pltpu.make_async_copy(source.at[pl.ds(total, TABLE_ROWS)], packed, w_sem.at[0])]
        for n in range(PIECES):
            at = pl.ds(n * piece, piece)
            copies.append(pltpu.make_async_copy(source.at[at], wts.at[at], w_sem.at[2 + n]))
        return copies

    in_copies = []
    for n in range(8):
        in_copies.append(
            pltpu.make_async_copy(
                got_ref.at[n],
                xs.at[
                    pl.ds((n // 4) * part_rows, part_rows), pl.ds((n % 4) * width, width)
                ],
                x_sem.at[n],
            )
        )
        in_copies[-1].start()
    for i in range(n_weights):

        @pl.when(chosen == i)
        def _(i=i):
            for one in weight_copies(sources[i]):
                one.start()

    waits = weight_copies(sources[0])
    waits[0].wait()
    wide[...] = packed[...].astype(jnp.float32).astype(jnp.int32)
    to_scalars = pltpu.make_async_copy(wide, table, w_sem.at[1])
    to_scalars.start()
    for one in in_copies:
        one.wait()
    to_scalars.wait()

    def block_product(source, rows, count, line, col, base):
        parts = []
        for i in range(count):
            at = pl.multiple_of(table[line + i, col] * blk, blk)
            parts.append(source[rows, pl.ds(at, blk)])
        return jnp.dot(
            jnp.concatenate(parts, axis=1),
            wts[base : base + count * blk, :],
            preferred_element_type=jnp.float32,
        )

    halves = [slice(0, part_rows), slice(part_rows, 2 * part_rows)]
    for col in range(up_cols):
        if (col * up_depth) % piece == 0:
            waits[1 + col * up_depth // piece].wait()
        for rows in halves:
            got = block_product(xs, rows, 2, 0, col, col * up_depth)
            hid[rows, col * blk : (col + 1) * blk] = gelu(got).astype(jnp.bfloat16)

    out_copies = []
    for col in range(down_cols):
        base = up_size + col * down_depth
        if base % piece == 0:
            waits[1 + base // piece].wait()
        for rows in halves:
            got = block_product(hid, rows, 4, 2, col, base)
            res[rows, col * blk : (col + 1) * blk] = got.astype(jnp.bfloat16)
        if (col + 1) % (down_cols // 2) == 0:
            half = (col + 1) // (down_cols // 2) - 1
            cols = pl.ds(half * (down_cols // 2) * blk, (down_cols // 2) * blk)
            share = cap // len(outs)
            for n in range(8 * len(outs)):
                owner, part = n // len(outs), n % len(outs)
                out_copies.append(
                    pltpu.make_async_copy(
                        res.at[pl.ds(owner * cap + part * share, share), cols],
                        outs[part].at[pl.ds(owner * share, share), cols],
                        o_sem.at[half * 8 * len(outs) + n],
                    )
                )
                out_copies[-1].start()
    for one in out_copies:
        one.wait()


def expert_rows(chosen, active, got, weights, hidden, cap, shares):
    _, part_rows, width = got.shape
    blk = weights[0].shape[1]
    rows, row_width = 2 * part_rows, 4 * width
    hbm = pl.BlockSpec(memory_space=pltpu.HBM)
    smem = pl.BlockSpec(memory_space=pltpu.SMEM)
    up_and_down = weights[0].shape[0] - TABLE_ROWS
    return pl.pallas_call(
        lambda *a: ffn_kernel(len(weights), cap, *a),
        in_specs=[smem] + [hbm] * (1 + len(weights)),
        out_specs=[hbm] * shares,
        out_shape=[jax.ShapeDtypeStruct((rows // shares, row_width), jnp.bfloat16)] * shares,
        scratch_shapes=[
            pltpu.VMEM((rows, row_width), jnp.bfloat16),
            pltpu.VMEM((up_and_down, blk), jnp.bfloat16),
            pltpu.VMEM((rows, hidden), jnp.bfloat16),
            pltpu.VMEM((rows, row_width), jnp.bfloat16),
            pltpu.VMEM((TABLE_ROWS, blk), jnp.bfloat16),
            pltpu.VMEM((TABLE_ROWS, blk), jnp.int32),
            pltpu.SMEM((TABLE_ROWS, blk), jnp.int32),
            pltpu.SemaphoreType.DMA((8,)),
            pltpu.SemaphoreType.DMA((2 + PIECES,)),
            pltpu.SemaphoreType.DMA((32,)),
        ],
        cost_estimate=pl.CostEstimate(
            flops=4 * rows * up_and_down * blk,
            bytes_accessed=12_000_000,
            transcendentals=rows * hidden,
        ),
        compiler_params=pltpu.CompilerParams(vmem_limit_bytes=60 * 2**20),
    )(jnp.stack([chosen, active]).astype(jnp.int32), got, *weights)


def gate_matrix(order, blocks, slots, choice_ref, gate_ref, high, low):
    tokens = choice_ref.shape[1]
    tops, rests = [], []
    for n, size, first in blocks:
        row = lax.broadcasted_iota(jnp.int32, (size, tokens), 0) + first
        line = slots[pl.ds(order[n], 1), :]
        gate = jnp.where(choice_ref[0:1, :] == order[n], gate_ref[0:1, :], gate_ref[1:2, :])
        top = gate.astype(jnp.bfloat16).astype(jnp.float32)
        here = line == row
        tops.append(jnp.where(here, top, 0.0).astype(jnp.bfloat16))
        rests.append(jnp.where(here, gate - top, 0.0).astype(jnp.bfloat16))
    high[...] = jnp.concatenate(tops, axis=0).T
    low[...] = jnp.concatenate(rests, axis=0).T


def first_kernel(experts, cap, order, choice_ref, gate_ref, rows_a, rows_1, sum_ref, *refs):
    high_b, low_b, slots, high, low, stack = refs
    part = cap // 2

    def of_core(on):
        return [(8 + 8 * (1 - on) + s, part, part * ((s % 2) ^ on)) for s in range(8)]

    @pl.when(pl.program_id(0) == 0)
    def _():
        slots[...] = slot_rows([(choice_ref[0:1, :], choice_ref[1:2, :])], experts)
        blocks = [(n, cap, 0) for n in range(8)] + of_core(1)
        gate_matrix(order, blocks, slots, choice_ref, gate_ref, high, low)
        gate_matrix(order, of_core(0), slots, choice_ref, gate_ref, high_b, low_b)

    stack[0 : 8 * cap, :] = rows_a[...]
    stack[8 * cap :, :] = rows_1[...]
    total = jnp.dot(high[...], stack[...], preferred_element_type=jnp.float32)
    total += jnp.dot(low[...], stack[...], preferred_element_type=jnp.float32)
    sum_ref[...] = total


def combine_first(order, choice, gates, rows_a, rows_1, experts, cap):
    tokens = choice.shape[1]
    row_width = rows_a.shape[1]
    count_a, count_1 = rows_a.shape[0], rows_1.shape[0]
    chunk = 512
    whole = pl.BlockSpec((2, tokens), lambda j, a: (0, 0))
    matrix = pl.BlockSpec((tokens, count_1), lambda j, a: (0, 0))
    return pl.pallas_call(
        lambda *a: first_kernel(experts, cap, *a),
        grid_spec=pltpu.PrefetchScalarGridSpec(
            num_scalar_prefetch=1,
            grid=(row_width // chunk,),
            in_specs=[
                whole,
                whole,
                pl.BlockSpec((count_a, chunk), lambda j, a: (0, j)),
                pl.BlockSpec((count_1, chunk), lambda j, a: (0, j)),
            ],
            out_specs=[pl.BlockSpec((tokens, chunk), lambda j, a: (0, j)), matrix, matrix],
            scratch_shapes=[
                pltpu.VMEM((experts, tokens), jnp.int32),
                pltpu.VMEM((tokens, count_a + count_1), jnp.bfloat16),
                pltpu.VMEM((tokens, count_a + count_1), jnp.bfloat16),
                pltpu.VMEM((count_a + count_1, chunk), jnp.bfloat16),
            ],
        ),
        out_shape=[jax.ShapeDtypeStruct((tokens, row_width), jnp.float32)]
        + [jax.ShapeDtypeStruct((tokens, count_1), jnp.bfloat16)] * 2,
        cost_estimate=pl.CostEstimate(
            flops=4 * (count_a + count_1) * tokens * row_width,
            bytes_accessed=9_000_000,
            transcendentals=0,
        ),
        compiler_params=pltpu.CompilerParams(vmem_limit_bytes=60 * 2**20),
    )(order, choice, gates, rows_a, rows_1)


def second_kernel(high, low, rows, sum_ref, out_ref):
    total = jnp.dot(high[...], rows[...], preferred_element_type=jnp.float32)
    total += jnp.dot(low[...], rows[...], preferred_element_type=jnp.float32)
    out_ref[...] = (total + sum_ref[...]).astype(out_ref.dtype)


def combine_second(high, low, rows, so_far):
    tokens, columns = high.shape
    row_width = rows.shape[1]
    chunk = 1024
    matrix = pl.BlockSpec((tokens, columns), lambda j: (0, 0))
    block = pl.BlockSpec((tokens, chunk), lambda j: (0, j))
    return pl.pallas_call(
        second_kernel,
        grid=(row_width // chunk,),
        in_specs=[matrix, matrix, pl.BlockSpec((columns, chunk), lambda j: (0, j)), block],
        out_specs=block,
        out_shape=jax.ShapeDtypeStruct((tokens, row_width), jnp.bfloat16),
        cost_estimate=pl.CostEstimate(
            flops=4 * columns * tokens * row_width, bytes_accessed=9_000_000, transcendentals=0
        ),
        compiler_params=pltpu.CompilerParams(vmem_limit_bytes=60 * 2**20),
    )(high, low, rows, so_far)


def per_device_planes(
    attention_rows, expert_choice, gate_weights, up_blocks, up_values, down_blocks, down_values
):
    experts = 2 * lax.axis_size("z") * lax.axis_size("x")
    own_tokens = expert_choice.shape[1]
    cap = 3 * own_tokens // experts
    blk = up_values.shape[-1]
    hidden = up_values.shape[1] * blk
    g, z = lax.axis_index("grp"), lax.axis_index("z")
    y, core = g // 2, g % 2
    features = attention_rows[0]

    own = pack_weights(
        y,
        up_values.reshape(2, -1, blk),
        down_values.reshape(2, -1, blk),
        up_blocks.transpose(0, 2, 1),
        down_blocks.transpose(0, 2, 1),
    )
    r1 = send(own, along_z(1, ((0, 0), (1, 1), (2, 1))))
    l1 = send(own, along_z(-1, ((3, 0), (2, 1), (1, 1))))

    choice = expert_choice[0].T
    gates = gate_weights[0].T
    choices = lax.all_gather(after(choice, own), "grp")
    planes = [place(jnp.int32(d % 2), z) for d in range(8)]
    bases = [2 * (d // 4) + d % 4 // 2 for d in range(8)]
    order_a = jnp.stack([4 * planes[d] + bases[d] for d in range(8)]).astype(jnp.int32)
    order_b = jnp.stack([4 * (3 - planes[d]) + bases[d] for d in range(8)]).astype(jnp.int32)
    rows_a = gather_rows(features, choices, order_a, experts, cap)
    got_a = exchange(rows_a)
    rows_b = gather_rows(features, after(choices, rows_a), order_b, experts, cap)
    r1, l1, rows_b = lax.optimization_barrier((r1, l1, rows_b))
    r2 = send(r1, along_z(1, ((1, 0), (2, 1))))
    l2 = send(l1, along_z(-1, ((2, 0), (1, 1))))
    got_a, rows_b = lax.optimization_barrier((got_a, rows_b))
    got_b = exchange(rows_b)

    pick = z * 2 + core
    take_a = jnp.array([0, 2, 1, 0, 2, 0, 0, 1], jnp.int32)[pick]
    (out_a,) = expert_rows(take_a, jnp.int32(1), got_a, (own, r1, l1), hidden, cap, 1)
    got_b, out_a = lax.optimization_barrier((got_b, out_a))
    back_a = exchange(out_a.reshape(8, cap, -1)).reshape(8 * cap, -1)
    r2, l2, out_a = lax.optimization_barrier((r2, l2, out_a))
    r3 = send(r2, along_z(1, ((2, 0),)))
    l3 = send(l2, along_z(-1, ((1, 0),)))

    def second(on, chosen, weights, earlier):
        keep, give = expert_rows(chosen[pick], core == on, got_b, weights, hidden, cap, 2)
        earlier, keep, give = lax.optimization_barrier((earlier, keep, give))
        taken = send(give, all_pairs(lambda y, c, z, x: (y, 1 - c, z, x) if c == on else None))
        return jnp.where(core == on, keep, taken), earlier

    def give_back(rows):
        return exchange(rows.reshape(8, cap // 2, -1)).reshape(4 * cap, -1)

    rows_1, _ = second(1, jnp.array([0, 3, 0, 1, 0, 2, 0, 0], jnp.int32), (r2, l1, r1, l2), ())
    back_a, rows_1 = lax.optimization_barrier((back_a, rows_1))
    back_1 = give_back(rows_1)
    r3, l3, got_b = lax.optimization_barrier((r3, l3, after(got_b, rows_1)))
    rows_0, back_1 = second(
        0, jnp.array([3, 0, 2, 0, 1, 0, 0, 0], jnp.int32), (r3, r2, l2, l3), back_1
    )
    back_0 = give_back(rows_0)
    order_c = [
        4 * (3 - place(jnp.int32(on), z)) + 2 * (s // 4) + s % 4 // 2
        for on in (1, 0)
        for s in range(8)
    ]
    order = jnp.concatenate([order_a, jnp.stack(order_c).astype(jnp.int32)])
    sum_a, high, low = combine_first(
        after(order, rows_0), choice, gates, back_a, back_1, experts, cap
    )
    return combine_second(high, low, back_0, sum_a)[None]


def expert_ffn(token_rows, up_rows, up_vals, down_rows, down_vals):
    row_count, row_width = token_rows.shape
    block_size = up_vals.shape[-1]
    in_blocks = row_width // block_size
    mid_blocks = up_rows.shape[0]
    pick_up = (up_rows[:, :, None] == jnp.arange(in_blocks)[None, None, :]).astype(jnp.bfloat16)
    chosen = jnp.einsum(
        "rnb,cin->rcib",
        token_rows.reshape(row_count, in_blocks, block_size),
        pick_up,
        preferred_element_type=jnp.float32,
    ).astype(jnp.bfloat16)
    hidden = jnp.einsum("rcib,cibd->rcd", chosen, up_vals, preferred_element_type=jnp.float32)
    hidden = jax.nn.gelu(hidden, approximate=True).astype(jnp.bfloat16)
    pick_down = (down_rows[:, :, None] == jnp.arange(mid_blocks)[None, None, :]).astype(
        jnp.bfloat16
    )
    chosen_mid = jnp.einsum(
        "rcb,jic->rjib", hidden, pick_down, preferred_element_type=jnp.float32
    ).astype(jnp.bfloat16)
    result = jnp.einsum("rjib,jibd->rjd", chosen_mid, down_vals, preferred_element_type=jnp.float32)
    return result.reshape(row_count, row_width).astype(jnp.bfloat16)


def padded_rows(all_rows, weights):
    total_rows, row_width = all_rows.shape
    tile_rows = math.gcd(total_rows, 128)
    tiles = all_rows.reshape(total_rows // tile_rows, tile_rows, row_width)
    mapped = lax.map(
        lambda tile_block: expert_ffn(tile_block, weights[0], weights[1], weights[2], weights[3]),
        tiles,
    )
    return mapped.reshape(total_rows, row_width)


def slot_targets(route_ids, expert_total, capacity):
    pair_ids = route_ids.reshape(-1)
    one_hot = (pair_ids[:, None] == jnp.arange(expert_total, dtype=jnp.int32)[None, :]).astype(
        jnp.int32
    )
    earlier = jnp.cumsum(one_hot, axis=0) - one_hot
    slot_number = jnp.sum(earlier * one_hot, axis=1)
    return (pair_ids * capacity + slot_number).reshape(route_ids.shape)


def place_rows(token_rows, targets, slot_total):
    buffer_rows = jnp.zeros((slot_total, token_rows.shape[1]), token_rows.dtype)
    buffer_rows = buffer_rows.at[targets[:, 0]].set(token_rows)
    return buffer_rows.at[targets[:, 1]].set(token_rows)


def per_device(
    attention_rows, expert_choice, gate_weights, up_blocks, up_values, down_blocks, down_values
):
    group_count = lax.axis_size("grp")
    expert_devices = lax.axis_size("exp")
    local_experts = up_values.shape[0]
    expert_total = local_experts * expert_devices
    own_tokens = expert_choice.shape[1]
    capacity = 3 * own_tokens // expert_total
    head_width = attention_rows.shape[2]
    row_width = head_width * group_count
    targets = slot_targets(expert_choice[0], expert_total, capacity)
    token_rows = lax.all_to_all(attention_rows, "grp", split_axis=1, concat_axis=2, tiled=True)[0]
    send_rows = place_rows(token_rows, targets, expert_total * capacity)
    send_rows = send_rows.reshape(expert_devices, local_experts, capacity, row_width)
    received = lax.all_to_all(send_rows, "exp", split_axis=0, concat_axis=0, tiled=True)
    outputs = []
    for local_index in range(local_experts):
        weights = (
            up_blocks[local_index],
            up_values[local_index],
            down_blocks[local_index],
            down_values[local_index],
        )
        expert_rows = received[:, local_index].reshape(expert_devices * capacity, row_width)
        expert_result = padded_rows(expert_rows, weights)
        outputs.append(expert_result.reshape(expert_devices, capacity, row_width))
    stacked = jnp.stack(outputs, axis=1)
    returned = lax.all_to_all(stacked, "exp", split_axis=0, concat_axis=0, tiled=True).reshape(
        expert_total * capacity, row_width
    )
    picked = returned[targets.reshape(-1)].reshape(own_tokens, 2, row_width)
    combined = jnp.sum(gate_weights[0][:, :, None] * picked.astype(jnp.float32), axis=1)
    return combined.astype(jnp.bfloat16)[None]


def solution(mesh):
    planes = mesh.shape["grp"] == 4 and mesh.shape["exp"] == 8
    exp = "exp"
    if planes:
        mesh = jax.sharding.Mesh(mesh.devices.reshape(4, 4, 2), AXES)
        exp = ("z", "x")
    return jax.shard_map(
        per_device_planes if planes else per_device,
        mesh=mesh,
        in_specs=(
            P(exp, None, "grp"),
            P(exp, "grp", None),
            P(exp, "grp", None),
            P(exp, None, None),
            P(exp, None, None, None, None),
            P(exp, None, None),
            P(exp, None, None, None, None),
        ),
        out_specs=P(exp, "grp", None),
        check_vma=False,
    )
```

```python
import functools
import math

import jax
import jax.numpy as jnp
import numpy as np
from jax import lax
from jax.experimental import pallas as pl
from jax.experimental.pallas import tpu as pltpu
from jax.sharding import PartitionSpec as P

AXES = ("grp", "z", "x")
PLANE = ("x", "grp")


def place(core, plane):
    return jnp.where(plane < 2, core, 3 - core)


def all_pairs(rule):
    pairs = []
    for y in range(2):
        for core in range(2):
            for z in range(4):
                for x in range(2):
                    to = rule(y, core, z, x)
                    if to is not None:
                        ty, tc, tz, tx = to
                        pairs.append(((y * 2 + core) * 8 + z * 2 + x, (ty * 2 + tc) * 8 + tz * 2 + tx))
    return pairs


def along_z(step, senders):
    return all_pairs(lambda y, c, z, x: (y, c, z + step, x) if (z, c) in senders else None)


def send(value, pairs):
    return lax.ppermute(value, AXES, pairs)


def after(value, other):
    return lax.optimization_barrier((value, other))[0]


PIECES = 2
TABLE_ROWS = 16


def pack_kernel(pieces, which, up, down, up_at, down_at, out, held, wide, rows, in_sem, out_sem):
    size = up.shape[1]
    step = size // pieces
    inward, outward = [], []
    for n in range(2 * pieces):
        source, at = (up, n * step) if n < pieces else (down, (n - pieces) * step)
        here = held.at[pl.ds(n * step, step)]
        inward.append(
            pltpu.make_async_copy(source.at[which[0], pl.ds(at, step)], here, in_sem.at[n])
        )
        outward.append(
            pltpu.make_async_copy(here, out.at[pl.ds(n * step, step)], out_sem.at[n])
        )
        inward[-1].start()
    ups, downs = up_at.shape[1], down_at.shape[1]
    wide[...] = jnp.zeros(wide.shape, jnp.float32)
    wide[0:ups, 0 : up_at.shape[2]] = up_at[which[0]].astype(jnp.float32)
    wide[ups : ups + downs, 0 : down_at.shape[2]] = down_at[which[0]].astype(jnp.float32)
    rows[...] = wide[...].astype(jnp.bfloat16)
    outward.append(
        pltpu.make_async_copy(rows, out.at[pl.ds(2 * size, TABLE_ROWS)], out_sem.at[2 * pieces])
    )
    outward[-1].start()
    for n in range(2 * pieces):
        inward[n].wait()
        outward[n].start()
    for one in outward:
        one.wait()


def pack_weights(which, up, down, up_at, down_at):
    pieces = 4
    size, blk = up.shape[1], up.shape[2]
    hbm = pl.BlockSpec(memory_space=pltpu.HBM)
    vmem = pl.BlockSpec(memory_space=pltpu.VMEM)
    return pl.pallas_call(
        lambda *a: pack_kernel(pieces, *a),
        in_specs=[pl.BlockSpec(memory_space=pltpu.SMEM), hbm, hbm, vmem, vmem],
        out_specs=hbm,
        out_shape=jax.ShapeDtypeStruct((2 * size + TABLE_ROWS, blk), up.dtype),
        scratch_shapes=[
            pltpu.VMEM((2 * size, blk), jnp.bfloat16),
            pltpu.VMEM((TABLE_ROWS, blk), jnp.float32),
            pltpu.VMEM((TABLE_ROWS, blk), jnp.bfloat16),
            pltpu.SemaphoreType.DMA((2 * pieces,)),
            pltpu.SemaphoreType.DMA((2 * pieces + 1,)),
        ],
        cost_estimate=pl.CostEstimate(flops=0, bytes_accessed=8_400_000, transcendentals=0),
        compiler_params=pltpu.CompilerParams(vmem_limit_bytes=60 * 2**20),
    )(which[None].astype(jnp.int32), up, down, up_at, down_at)


def slot_rows(pairs, experts):
    tokens = pairs[0][0].shape[1]
    ids = lax.broadcasted_iota(jnp.int32, (experts, tokens), 0)
    named = [jnp.where((ids == a) | (ids == b), 1.0, 0.0) for a, b in pairs]
    named = jnp.concatenate(named, axis=0)
    before = lax.broadcasted_iota(jnp.int32, (tokens, tokens), 0) < lax.broadcasted_iota(
        jnp.int32, (tokens, tokens), 1
    )
    count = jnp.dot(
        named.astype(jnp.bfloat16),
        jnp.where(before, 1.0, 0.0).astype(jnp.bfloat16),
        preferred_element_type=jnp.float32,
    )
    return jnp.where(named > 0.5, count.astype(jnp.int32), -1)


def exchange(rows):
    return lax.all_to_all(rows, PLANE, split_axis=0, concat_axis=0, tiled=True)


def gather_kernel(experts, cap, order, x_ref, choice_ref, out_ref, slots, pick):
    tokens = x_ref.shape[0]
    part = pl.program_id(0)

    @pl.when(part == 0)
    def _():
        pairs = [(choice_ref[b, 0:1, :], choice_ref[b, 1:2, :]) for b in range(choice_ref.shape[0])]
        slots[...] = slot_rows(pairs, experts)

    row = lax.broadcasted_iota(jnp.int32, (cap, tokens), 0)
    for n in range(8):
        line = slots[pl.ds(part * experts + order[n], 1), :]
        pick[n * cap : (n + 1) * cap, :] = jnp.where(line == row, 1.0, 0.0).astype(jnp.bfloat16)
    for n in range(0, 8, 2):
        rows = jnp.dot(
            pick[n * cap : (n + 2) * cap, :], x_ref[...], preferred_element_type=jnp.float32
        )
        out_ref[n] = rows[:cap].astype(jnp.bfloat16)
        out_ref[n + 1] = rows[cap:].astype(jnp.bfloat16)


def gather_rows(features, choices, order, experts, cap):
    parts, _, tokens = choices.shape
    width = features.shape[1]
    return pl.pallas_call(
        lambda *a: gather_kernel(experts, cap, *a),
        grid_spec=pltpu.PrefetchScalarGridSpec(
            num_scalar_prefetch=1,
            grid=(parts,),
            in_specs=[
                pl.BlockSpec((tokens, width), lambda b, order: (b, 0)),
                pl.BlockSpec((parts, 2, tokens), lambda b, order: (0, 0, 0)),
            ],
            out_specs=pl.BlockSpec((8, cap, width), lambda b, order: (0, b, 0)),
            scratch_shapes=[
                pltpu.VMEM((parts * experts, tokens), jnp.int32),
                pltpu.VMEM((8 * cap, tokens), jnp.bfloat16),
            ],
        ),
        out_shape=jax.ShapeDtypeStruct((8, parts * cap, width), jnp.bfloat16),
        cost_estimate=pl.CostEstimate(
            flops=2 * parts * 8 * cap * tokens * width, bytes_accessed=9_000_000, transcendentals=0
        ),
        compiler_params=pltpu.CompilerParams(vmem_limit_bytes=60 * 2**20),
    )(order, features, choices)


def gelu(v):
    half = 0.5 * v
    inner = v * (math.sqrt(2 / math.pi) + (math.sqrt(2 / math.pi) * 0.044715) * (v * v))
    return half + half * jnp.tanh(inner)


def ffn_kernel(n_weights, cap, meta, *refs):
    @pl.when(meta[1] == 1)
    def _():
        run_expert(n_weights, cap, meta[0], *refs)


def run_expert(n_weights, cap, chosen, got_ref, *refs):
    sources, refs = refs[:n_weights], refs[n_weights:]
    outs, refs = refs[:-10], refs[-10:]
    xs, wts, hid, res, packed, wide, table, x_sem, w_sem, o_sem = refs
    part_rows, width = got_ref.shape[1], got_ref.shape[2]
    blk = wts.shape[1]
    up_cols = hid.shape[1] // blk
    down_cols = res.shape[1] // blk
    up_depth, down_depth = 2 * blk, 4 * blk
    up_size = up_cols * up_depth

    total = up_size + down_cols * down_depth
    piece = total // PIECES

    def weight_copies(source):
        copies = [pltpu.make_async_copy(source.at[pl.ds(total, TABLE_ROWS)], packed, w_sem.at[0])]
        for n in range(PIECES):
            at = pl.ds(n * piece, piece)
            copies.append(pltpu.make_async_copy(source.at[at], wts.at[at], w_sem.at[2 + n]))
        return copies

    in_copies = []
    for n in range(8):
        in_copies.append(
            pltpu.make_async_copy(
                got_ref.at[n],
                xs.at[
                    pl.ds((n // 4) * part_rows, part_rows), pl.ds((n % 4) * width, width)
                ],
                x_sem.at[n],
            )
        )
        in_copies[-1].start()
    for i in range(n_weights):

        @pl.when(chosen == i)
        def _(i=i):
            for one in weight_copies(sources[i]):
                one.start()

    waits = weight_copies(sources[0])
    waits[0].wait()
    wide[...] = packed[...].astype(jnp.float32).astype(jnp.int32)
    to_scalars = pltpu.make_async_copy(wide, table, w_sem.at[1])
    to_scalars.start()
    for one in in_copies:
        one.wait()
    to_scalars.wait()

    def block_product(source, rows, count, line, col, base):
        parts = []
        for i in range(count):
            at = pl.multiple_of(table[line + i, col] * blk, blk)
            parts.append(source[rows, pl.ds(at, blk)])
        return jnp.dot(
            jnp.concatenate(parts, axis=1),
            wts[base : base + count * blk, :],
            preferred_element_type=jnp.float32,
        )

    halves = [slice(0, part_rows), slice(part_rows, 2 * part_rows)]
    for col in range(up_cols):
        if (col * up_depth) % piece == 0:
            waits[1 + col * up_depth // piece].wait()
        for rows in halves:
            got = block_product(xs, rows, 2, 0, col, col * up_depth)
            hid[rows, col * blk : (col + 1) * blk] = gelu(got).astype(jnp.bfloat16)

    out_copies = []
    for col in range(down_cols):
        base = up_size + col * down_depth
        if base % piece == 0:
            waits[1 + base // piece].wait()
        for rows in halves:
            got = block_product(hid, rows, 4, 2, col, base)
            res[rows, col * blk : (col + 1) * blk] = got.astype(jnp.bfloat16)
        if (col + 1) % (down_cols // 2) == 0:
            half = (col + 1) // (down_cols // 2) - 1
            cols = pl.ds(half * (down_cols // 2) * blk, (down_cols // 2) * blk)
            share = cap // len(outs)
            for n in range(8 * len(outs)):
                owner, part = n // len(outs), n % len(outs)
                out_copies.append(
                    pltpu.make_async_copy(
                        res.at[pl.ds(owner * cap + part * share, share), cols],
                        outs[part].at[pl.ds(owner * share, share), cols],
                        o_sem.at[half * 8 * len(outs) + n],
                    )
                )
                out_copies[-1].start()
    for one in out_copies:
        one.wait()


def expert_rows(chosen, active, got, weights, hidden, cap, shares):
    _, part_rows, width = got.shape
    blk = weights[0].shape[1]
    rows, row_width = 2 * part_rows, 4 * width
    hbm = pl.BlockSpec(memory_space=pltpu.HBM)
    smem = pl.BlockSpec(memory_space=pltpu.SMEM)
    up_and_down = weights[0].shape[0] - TABLE_ROWS
    return pl.pallas_call(
        lambda *a: ffn_kernel(len(weights), cap, *a),
        in_specs=[smem] + [hbm] * (1 + len(weights)),
        out_specs=[hbm] * shares,
        out_shape=[jax.ShapeDtypeStruct((rows // shares, row_width), jnp.bfloat16)] * shares,
        scratch_shapes=[
            pltpu.VMEM((rows, row_width), jnp.bfloat16),
            pltpu.VMEM((up_and_down, blk), jnp.bfloat16),
            pltpu.VMEM((rows, hidden), jnp.bfloat16),
            pltpu.VMEM((rows, row_width), jnp.bfloat16),
            pltpu.VMEM((TABLE_ROWS, blk), jnp.bfloat16),
            pltpu.VMEM((TABLE_ROWS, blk), jnp.int32),
            pltpu.SMEM((TABLE_ROWS, blk), jnp.int32),
            pltpu.SemaphoreType.DMA((8,)),
            pltpu.SemaphoreType.DMA((2 + PIECES,)),
            pltpu.SemaphoreType.DMA((32,)),
        ],
        cost_estimate=pl.CostEstimate(
            flops=4 * rows * up_and_down * blk,
            bytes_accessed=12_000_000,
            transcendentals=rows * hidden,
        ),
        compiler_params=pltpu.CompilerParams(vmem_limit_bytes=60 * 2**20),
    )(jnp.stack([chosen, active]).astype(jnp.int32), got, *weights)


def gate_matrix(order, blocks, slots, choice_ref, gate_ref, high, low):
    tokens = choice_ref.shape[1]
    tops, rests = [], []
    for n, size, first in blocks:
        row = lax.broadcasted_iota(jnp.int32, (size, tokens), 0) + first
        line = slots[pl.ds(order[n], 1), :]
        gate = jnp.where(choice_ref[0:1, :] == order[n], gate_ref[0:1, :], gate_ref[1:2, :])
        top = gate.astype(jnp.bfloat16).astype(jnp.float32)
        here = line == row
        tops.append(jnp.where(here, top, 0.0).astype(jnp.bfloat16))
        rests.append(jnp.where(here, gate - top, 0.0).astype(jnp.bfloat16))
    high[...] = jnp.concatenate(tops, axis=0).T
    low[...] = jnp.concatenate(rests, axis=0).T


def first_kernel(experts, cap, order, choice_ref, gate_ref, rows_a, rows_1, sum_ref, *refs):
    high_b, low_b, slots, high, low, stack = refs
    part = cap // 2

    def of_core(on):
        return [(8 + 8 * (1 - on) + s, part, part * ((s % 2) ^ on)) for s in range(8)]

    @pl.when(pl.program_id(0) == 0)
    def _():
        slots[...] = slot_rows([(choice_ref[0:1, :], choice_ref[1:2, :])], experts)
        blocks = [(n, cap, 0) for n in range(8)] + of_core(1)
        gate_matrix(order, blocks, slots, choice_ref, gate_ref, high, low)
        gate_matrix(order, of_core(0), slots, choice_ref, gate_ref, high_b, low_b)

    stack[0 : 8 * cap, :] = rows_a[...]
    stack[8 * cap :, :] = rows_1[...]
    total = jnp.dot(high[...], stack[...], preferred_element_type=jnp.float32)
    total += jnp.dot(low[...], stack[...], preferred_element_type=jnp.float32)
    sum_ref[...] = total


def combine_first(order, choice, gates, rows_a, rows_1, experts, cap):
    tokens = choice.shape[1]
    row_width = rows_a.shape[1]
    count_a, count_1 = rows_a.shape[0], rows_1.shape[0]
    chunk = 512
    whole = pl.BlockSpec((2, tokens), lambda j, a: (0, 0))
    matrix = pl.BlockSpec((tokens, count_1), lambda j, a: (0, 0))
    return pl.pallas_call(
        lambda *a: first_kernel(experts, cap, *a),
        grid_spec=pltpu.PrefetchScalarGridSpec(
            num_scalar_prefetch=1,
            grid=(row_width // chunk,),
            in_specs=[
                whole,
                whole,
                pl.BlockSpec((count_a, chunk), lambda j, a: (0, j)),
                pl.BlockSpec((count_1, chunk), lambda j, a: (0, j)),
            ],
            out_specs=[pl.BlockSpec((tokens, chunk), lambda j, a: (0, j)), matrix, matrix],
            scratch_shapes=[
                pltpu.VMEM((experts, tokens), jnp.int32),
                pltpu.VMEM((tokens, count_a + count_1), jnp.bfloat16),
                pltpu.VMEM((tokens, count_a + count_1), jnp.bfloat16),
                pltpu.VMEM((count_a + count_1, chunk), jnp.bfloat16),
            ],
        ),
        out_shape=[jax.ShapeDtypeStruct((tokens, row_width), jnp.float32)]
        + [jax.ShapeDtypeStruct((tokens, count_1), jnp.bfloat16)] * 2,
        cost_estimate=pl.CostEstimate(
            flops=4 * (count_a + count_1) * tokens * row_width,
            bytes_accessed=9_000_000,
            transcendentals=0,
        ),
        compiler_params=pltpu.CompilerParams(vmem_limit_bytes=60 * 2**20),
    )(order, choice, gates, rows_a, rows_1)


def second_kernel(high, low, rows, sum_ref, out_ref):
    total = jnp.dot(high[...], rows[...], preferred_element_type=jnp.float32)
    total += jnp.dot(low[...], rows[...], preferred_element_type=jnp.float32)
    out_ref[...] = (total + sum_ref[...]).astype(out_ref.dtype)


def combine_second(high, low, rows, so_far):
    tokens, columns = high.shape
    row_width = rows.shape[1]
    chunk = 1024
    matrix = pl.BlockSpec((tokens, columns), lambda j: (0, 0))
    block = pl.BlockSpec((tokens, chunk), lambda j: (0, j))
    return pl.pallas_call(
        second_kernel,
        grid=(row_width // chunk,),
        in_specs=[matrix, matrix, pl.BlockSpec((columns, chunk), lambda j: (0, j)), block],
        out_specs=block,
        out_shape=jax.ShapeDtypeStruct((tokens, row_width), jnp.bfloat16),
        cost_estimate=pl.CostEstimate(
            flops=4 * columns * tokens * row_width, bytes_accessed=9_000_000, transcendentals=0
        ),
        compiler_params=pltpu.CompilerParams(vmem_limit_bytes=60 * 2**20),
    )(high, low, rows, so_far)


def per_device_planes(
    attention_rows, expert_choice, gate_weights, up_blocks, up_values, down_blocks, down_values
):
    experts = 2 * lax.axis_size("z") * lax.axis_size("x")
    own_tokens = expert_choice.shape[1]
    cap = 3 * own_tokens // experts
    blk = up_values.shape[-1]
    hidden = up_values.shape[1] * blk
    g, z = lax.axis_index("grp"), lax.axis_index("z")
    y, core = g // 2, g % 2
    features = attention_rows[0]

    own = pack_weights(
        y,
        up_values.reshape(2, -1, blk),
        down_values.reshape(2, -1, blk),
        up_blocks.transpose(0, 2, 1),
        down_blocks.transpose(0, 2, 1),
    )
    r1 = send(own, along_z(1, ((0, 0), (1, 1), (2, 1))))
    l1 = send(own, along_z(-1, ((3, 0), (2, 1), (1, 1))))

    choice = expert_choice[0].T
    gates = gate_weights[0].T
    choices = lax.all_gather(after(choice, own), "grp")
    planes = [place(jnp.int32(d % 2), z) for d in range(8)]
    bases = [2 * (d // 4) + d % 4 // 2 for d in range(8)]
    order_a = jnp.stack([4 * planes[d] + bases[d] for d in range(8)]).astype(jnp.int32)
    order_b = jnp.stack([4 * (3 - planes[d]) + bases[d] for d in range(8)]).astype(jnp.int32)
    rows_a = gather_rows(features, choices, order_a, experts, cap)
    got_a = exchange(rows_a)
    rows_b = gather_rows(features, after(choices, rows_a), order_b, experts, cap)
    r1, l1, rows_b = lax.optimization_barrier((r1, l1, rows_b))
    r2 = send(r1, along_z(1, ((1, 0), (2, 1))))
    l2 = send(l1, along_z(-1, ((2, 0), (1, 1))))
    got_a, rows_b = lax.optimization_barrier((got_a, rows_b))
    got_b = exchange(rows_b)

    pick = z * 2 + core
    take_a = jnp.array([0, 2, 1, 0, 2, 0, 0, 1], jnp.int32)[pick]
    (out_a,) = expert_rows(take_a, jnp.int32(1), got_a, (own, r1, l1), hidden, cap, 1)
    got_b, out_a = lax.optimization_barrier((got_b, out_a))
    back_a = exchange(out_a.reshape(8, cap, -1)).reshape(8 * cap, -1)
    r2, l2, out_a = lax.optimization_barrier((r2, l2, out_a))
    r3 = send(r2, along_z(1, ((2, 0),)))
    l3 = send(l2, along_z(-1, ((1, 0),)))

    def second(on, chosen, weights, earlier):
        keep, give = expert_rows(chosen[pick], core == on, got_b, weights, hidden, cap, 2)
        earlier, keep, give = lax.optimization_barrier((earlier, keep, give))
        taken = send(give, all_pairs(lambda y, c, z, x: (y, 1 - c, z, x) if c == on else None))
        return jnp.where(core == on, keep, taken), earlier

    def give_back(rows):
        return exchange(rows.reshape(8, cap // 2, -1)).reshape(4 * cap, -1)

    rows_1, _ = second(1, jnp.array([0, 3, 0, 1, 0, 2, 0, 0], jnp.int32), (r2, l1, r1, l2), ())
    back_a, rows_1 = lax.optimization_barrier((back_a, rows_1))
    back_1 = give_back(rows_1)
    r3, l3, got_b = lax.optimization_barrier((r3, l3, after(got_b, rows_1)))
    rows_0, back_1 = second(
        0, jnp.array([3, 0, 2, 0, 1, 0, 0, 0], jnp.int32), (r3, r2, l2, l3), back_1
    )
    back_0 = give_back(rows_0)
    order_c = [
        4 * (3 - place(jnp.int32(on), z)) + 2 * (s // 4) + s % 4 // 2
        for on in (1, 0)
        for s in range(8)
    ]
    order = jnp.concatenate([order_a, jnp.stack(order_c).astype(jnp.int32)])
    sum_a, high, low = combine_first(
        after(order, rows_0), choice, gates, back_a, back_1, experts, cap
    )
    return combine_second(high, low, back_0, sum_a)[None]


def expert_ffn(token_rows, up_rows, up_vals, down_rows, down_vals):
    row_count, row_width = token_rows.shape
    block_size = up_vals.shape[-1]
    in_blocks = row_width // block_size
    mid_blocks = up_rows.shape[0]
    pick_up = (up_rows[:, :, None] == jnp.arange(in_blocks)[None, None, :]).astype(jnp.bfloat16)
    chosen = jnp.einsum(
        "rnb,cin->rcib",
        token_rows.reshape(row_count, in_blocks, block_size),
        pick_up,
        preferred_element_type=jnp.float32,
    ).astype(jnp.bfloat16)
    hidden = jnp.einsum("rcib,cibd->rcd", chosen, up_vals, preferred_element_type=jnp.float32)
    hidden = jax.nn.gelu(hidden, approximate=True).astype(jnp.bfloat16)
    pick_down = (down_rows[:, :, None] == jnp.arange(mid_blocks)[None, None, :]).astype(
        jnp.bfloat16
    )
    chosen_mid = jnp.einsum(
        "rcb,jic->rjib", hidden, pick_down, preferred_element_type=jnp.float32
    ).astype(jnp.bfloat16)
    result = jnp.einsum("rjib,jibd->rjd", chosen_mid, down_vals, preferred_element_type=jnp.float32)
    return result.reshape(row_count, row_width).astype(jnp.bfloat16)


def padded_rows(all_rows, weights):
    total_rows, row_width = all_rows.shape
    tile_rows = math.gcd(total_rows, 128)
    tiles = all_rows.reshape(total_rows // tile_rows, tile_rows, row_width)
    mapped = lax.map(
        lambda tile_block: expert_ffn(tile_block, weights[0], weights[1], weights[2], weights[3]),
        tiles,
    )
    return mapped.reshape(total_rows, row_width)


def slot_targets(route_ids, expert_total, capacity):
    pair_ids = route_ids.reshape(-1)
    one_hot = (pair_ids[:, None] == jnp.arange(expert_total, dtype=jnp.int32)[None, :]).astype(
        jnp.int32
    )
    earlier = jnp.cumsum(one_hot, axis=0) - one_hot
    slot_number = jnp.sum(earlier * one_hot, axis=1)
    return (pair_ids * capacity + slot_number).reshape(route_ids.shape)


def place_rows(token_rows, targets, slot_total):
    buffer_rows = jnp.zeros((slot_total, token_rows.shape[1]), token_rows.dtype)
    buffer_rows = buffer_rows.at[targets[:, 0]].set(token_rows)
    return buffer_rows.at[targets[:, 1]].set(token_rows)


def per_device(
    attention_rows, expert_choice, gate_weights, up_blocks, up_values, down_blocks, down_values
):
    group_count = lax.axis_size("grp")
    expert_devices = lax.axis_size("exp")
    local_experts = up_values.shape[0]
    expert_total = local_experts * expert_devices
    own_tokens = expert_choice.shape[1]
    capacity = 3 * own_tokens // expert_total
    head_width = attention_rows.shape[2]
    row_width = head_width * group_count
    targets = slot_targets(expert_choice[0], expert_total, capacity)
    token_rows = lax.all_to_all(attention_rows, "grp", split_axis=1, concat_axis=2, tiled=True)[0]
    send_rows = place_rows(token_rows, targets, expert_total * capacity)
    send_rows = send_rows.reshape(expert_devices, local_experts, capacity, row_width)
    received = lax.all_to_all(send_rows, "exp", split_axis=0, concat_axis=0, tiled=True)
    outputs = []
    for local_index in range(local_experts):
        weights = (
            up_blocks[local_index],
            up_values[local_index],
            down_blocks[local_index],
            down_values[local_index],
        )
        expert_rows = received[:, local_index].reshape(expert_devices * capacity, row_width)
        expert_result = padded_rows(expert_rows, weights)
        outputs.append(expert_result.reshape(expert_devices, capacity, row_width))
    stacked = jnp.stack(outputs, axis=1)
    returned = lax.all_to_all(stacked, "exp", split_axis=0, concat_axis=0, tiled=True).reshape(
        expert_total * capacity, row_width
    )
    picked = returned[targets.reshape(-1)].reshape(own_tokens, 2, row_width)
    combined = jnp.sum(gate_weights[0][:, :, None] * picked.astype(jnp.float32), axis=1)
    return combined.astype(jnp.bfloat16)[None]


def solution(mesh):
    planes = mesh.shape["grp"] == 4 and mesh.shape["exp"] == 8
    exp = "exp"
    if planes:
        mesh = jax.sharding.Mesh(mesh.devices.reshape(4, 4, 2), AXES)
        exp = ("z", "x")
    return jax.shard_map(
        per_device_planes if planes else per_device,
        mesh=mesh,
        in_specs=(
            P(exp, None, "grp"),
            P(exp, "grp", None),
            P(exp, "grp", None),
            P(exp, None, None),
            P(exp, None, None, None, None),
            P(exp, None, None),
            P(exp, None, None, None, None),
        ),
        out_specs=P(exp, "grp", None),
        check_vma=False,
    )
```
